32 devices in a mesh: experts: 4 (over z), context: 4 (over y, x), dp: 2 (over core).
Axes of the slice: x: 2, y: 2, z: 4, core: 2. Of those that a mesh axis runs over, the one named last changes fastest.
Arguments:
- tokens: bfloat16 [8, 1024, 768], P(('experts', 'dp'), 'context'), may hold values from -6 to 6
- cotangent: bfloat16 [8, 1024, 768], P(('experts', 'dp'), 'context'), may hold values from -6 to 6
- w_query: bfloat16 [768, 768], replicated, may hold values from -0.0546875 to 0.0546875
- w_key: bfloat16 [768, 768], replicated, may hold values from -0.21875 to 0.21875
- w_value: bfloat16 [768, 768], replicated, may hold values from -0.21875 to 0.21875
- w_output: bfloat16 [768, 768], replicated, may hold values from -1.75 to 1.75
- gain_attn: float32 [768], replicated, may hold values from 0.5 to 1.5
- gain_ffn: float32 [768], replicated, may hold values from 0.5 to 1.5
- bias_table: float32 [32, 12], replicated, may hold values from -4 to 4
- w_router: float32 [768, 8], replicated, may hold values from -0.15625 to 0.15625
- w_in: bfloat16 [8, 768, 3072], P('experts'), may hold values from -0.21875 to 0.21875
- w_out: bfloat16 [8, 3072, 768], P('experts'), may hold values from -3 to 3
- routes: int32 [8, 1024], P(('experts', 'dp'), 'context'), may hold values from 0 to 7
- slots: int32 [8, 1024], P(('experts', 'dp'), 'context'), may hold values from 0 to 95, as said below
- buckets: int32 [2047], replicated, may hold values from 0 to 31, as said below
Outputs:
- output: bfloat16 [8, 1024, 768], P(('experts', 'dp'), 'context')
- grad_tokens: float32 [8, 1024, 768], P(('experts', 'dp'), 'context')
- grad_query: float32 [768, 768], replicated
- grad_key: float32 [768, 768], replicated
- grad_value: float32 [768, 768], replicated
- grad_output: float32 [768, 768], replicated
- grad_gain_attn: float32 [768], replicated
- grad_gain_ffn: float32 [768], replicated
- grad_table: float32 [32, 12], replicated
- grad_router: float32 [768, 8], replicated
- grad_w_in: float32 [8, 768, 3072], P('experts', None, ('context', 'dp'))
- grad_w_out: float32 [8, 3072, 768], P('experts', ('context', 'dp'))
The draws below stay inside these ranges and needn't reach their ends.
Inputs may be any that keep to these rules, and one draw needn't show every extreme that they name: Within one device's 256 tokens (aligned blocks of one sequence), the tokens routed to one expert hold distinct slots; a token whose slot is 64 or more is dropped from its expert. `buckets`: entry r + 1023 holds the bucket of the offset r = key position minus query position: under 32 // 2 for r <= 0 and 16 or more for r > 0; it does not fall as |r| grows on each side.
All inputs are finite; a program needn't handle non-finite values.
Results may differ from the reference program's by a relative error of at most 0.015.
The reference program's roundings to bfloat16 on the way count: a program that leaves them out, or rounds other values in their place, can miss the bound.
Values may be sent and summed in bfloat16 or wider, within the bound.
A program may use at most 192 MiB of HBM per device.

```python
import jax
import jax.numpy as jnp
from jax import lax

D = 768
HEADS = 12
HEAD_DIM = 64
FF = 3072
BUCKETS = 32
TOK_DEV = 256
LEN = 1024
SEQS = 8
EXPERTS = 8
CAP = 64
N_CONTEXT = 4
N_DP = 2


def route_pool(key):
    blocks = SEQS * N_CONTEXT
    per_expert = CAP + CAP // 2
    pool = EXPERTS * per_expert
    key_pop, key_forced, key_noise, key_perm = jax.random.split(key, 4)
    popular = jax.random.randint(key_pop, (blocks, EXPERTS), 0, 4)
    forced_table = jax.random.randint(key_forced, (N_CONTEXT * N_DP,), 0, EXPERTS)
    block_ids = jnp.arange(blocks)
    group = block_ids % N_CONTEXT * N_DP + block_ids // N_CONTEXT % N_DP
    forced = forced_table[group]
    pool_ids = jnp.arange(pool)
    owner = pool_ids // per_expert
    position = pool_ids % per_expert
    prefer = (per_expert - 1 - position) * 8192 // per_expert
    noise = jax.random.randint(key_noise, (blocks, pool), 0, 4096)
    coarse = (owner[None, :] == forced[:, None]).astype(jnp.int32) * 65536 + popular[:, owner] * 2048 + prefer[None, :] + noise
    score = coarse * pool + pool_ids[None, :]
    chosen = lax.top_k(score, TOK_DEV)[1]

    def shuffle(block_key):
        return jax.random.permutation(block_key, TOK_DEV)
    orders = jax.vmap(shuffle)(jax.random.split(key_perm, blocks))
    selected_expert = jnp.take_along_axis(chosen, orders, axis=1)
    return (owner[selected_expert].reshape(SEQS, LEN).astype(jnp.int32), position[selected_expert].reshape(SEQS, LEN).astype(jnp.int32))


def draw_routes(key, part):
    return route_pool(key)[0]


def draw_slots(key, part):
    return route_pool(key)[1]


def draw_buckets(key, part):
    key = jax.random.fold_in(key, 7)
    half = BUCKETS // 2
    exact = half // 2
    levels_count = half - exact
    levels = jnp.arange(1, levels_count)
    base = jnp.maximum(exact + levels, LEN * 2 ** levels // 2 ** (levels_count + 1))
    jitter = jax.random.randint(key, (levels_count - 1,), 0, 1048576) % jnp.maximum(base // 2, 1)
    bounds = base + jitter
    offset = jnp.arange(2 * LEN - 1) - (LEN - 1)
    distance = jnp.abs(offset)
    far_bucket = exact + jnp.sum((distance[:, None] >= bounds[None, :]).astype(jnp.int32), axis=1)
    bucket = jnp.where(distance < exact, distance, far_bucket) + half * (offset > 0).astype(jnp.int32)
    return bucket.astype(jnp.int32)


def shard_levels(stream_key, dims, pieces, low, top_value):
    def one(axis_at, shards_of):
        heights = jax.random.uniform(jax.random.fold_in(jax.random.fold_in(stream_key, 6), axis_at), (shards_of,), jnp.float32, low / len(pieces), top_value / len(pieces))
        return jnp.repeat(jnp.exp(heights), dims[axis_at] // shards_of).reshape((-1,) + (1,) * (len(dims) - axis_at - 1))

    level = one(*pieces[0])
    for cut in pieces[1:]:
        level = level * one(*cut)
    return level


def gaussian(own_key, dims, width, limit, pieces=(), held_as=jnp.bfloat16):
    values = jax.random.normal(own_key, dims, jnp.float32) * width
    if len(pieces) > 0:
        values = shard_levels(own_key, dims, pieces, -0.22, 0.18) * values
    return jnp.clip(values, min=-limit, max=limit).astype(held_as)


def setup_inputs(seed: int = 0) -> dict:
    streams_of = jax.random.split(jax.random.key(seed), 16)
    return {
        "tokens": gaussian(streams_of[0], (SEQS, LEN, D), 1.0, 6.0, ((0, 8), (1, 4))),
        "cotangent": gaussian(streams_of[1], (SEQS, LEN, D), 1.0, 6.0, ((0, 8), (1, 4))),
        "w_query": gaussian(streams_of[2], (D, D), (16 * D) ** -0.5, 0.0546875),
        "w_key": gaussian(streams_of[3], (D, D), D ** -0.5, 0.21875),
        "w_value": gaussian(streams_of[4], (D, D), D ** -0.5, 0.21875),
        "w_output": gaussian(streams_of[5], (D, D), (D // 64) ** -0.5, 1.75),
        "gain_attn": jnp.clip(1.0 + 0.1 * jax.random.normal(streams_of[6], (D,), jnp.float32), 0.5, 1.5),
        "gain_ffn": jnp.clip(1.0 + 0.1 * jax.random.normal(streams_of[7], (D,), jnp.float32), 0.5, 1.5),
        "bias_table": gaussian(streams_of[8], (BUCKETS, HEADS), 1.0, 4.0, (), jnp.float32),
        "w_router": gaussian(streams_of[9], (D, EXPERTS), (2 * D) ** -0.5, 0.15625, (), jnp.float32),
        "w_in": gaussian(streams_of[10], (EXPERTS, D, FF), D ** -0.5, 0.21875, ((0, 4),)),
        "w_out": gaussian(streams_of[11], (EXPERTS, FF, D), (0.025 * EXPERTS), 3.0, ((0, 4),)),
        "routes": draw_routes(jax.random.fold_in(streams_of[15], 71), 0),
        "slots": draw_slots(jax.random.fold_in(streams_of[15], 71), 0),
        "buckets": draw_buckets(jax.random.fold_in(streams_of[15], 71), 0),
    }


@jax.custom_vjp
def low(v):
    return lax.optimization_barrier(v.astype(jnp.bfloat16)).astype(jnp.float32)

@jax.custom_vjp
def low_back(v):
    return v

def low_keep(v):
    return (low(v), None)

def low_pass(kept, grad):
    return (grad,)

def back_keep(v):
    return (v, None)

def back_low(kept, grad):
    return (low(grad),)
low.defvjp(low_keep, low_pass)
low_back.defvjp(back_keep, back_low)

def rms_scale(value_rows, gain):
    return value_rows * lax.rsqrt(lax.optimization_barrier(jnp.mean(value_rows * value_rows, axis=-1, keepdims=True)) + 1e-06) * gain

def dot_high(left, right):
    return jnp.dot(left, right, precision=lax.Precision.HIGHEST)

def project(value_rows, weight_matrix):
    return jnp.einsum('boc,cm->bom', value_rows, weight_matrix, precision=lax.Precision.HIGHEST)

def reference(tokens, cotangent, w_query, w_key, w_value, w_output, gain_attn, gain_ffn, bias_table, w_router, w_in, w_out, routes, slots, buckets):
    blocks = SEQS * N_CONTEXT
    one_hot = (buckets[:, None] == jnp.arange(BUCKETS, dtype=jnp.int32)[None, :]).astype(jnp.float32)
    offsets = (jnp.arange(LEN, dtype=jnp.int32)[None, :] - jnp.arange(LEN, dtype=jnp.int32)[:, None] + LEN - 1).astype(jnp.int32)
    route_blocks = routes.reshape(blocks, TOK_DEV)
    slot_blocks = slots.reshape(blocks, TOK_DEV)
    kept = slot_blocks < CAP
    layout = route_blocks * CAP + slot_blocks
    target = jnp.where(kept, layout, EXPERTS * CAP).astype(jnp.int32)
    read_index = jnp.where(kept, layout, 0).astype(jnp.int32)

    def fill_slots(target_row):
        table = jnp.full((EXPERTS * CAP + 1,), TOK_DEV, jnp.int32)
        return table.at[target_row].set(jnp.arange(TOK_DEV, dtype=jnp.int32))[:-1]
    slot_token = jax.vmap(fill_slots)(target)
    route_hot = (routes[..., None] == jnp.arange(EXPERTS, dtype=jnp.int32)).astype(jnp.float32)

    def forward(resid, wq, wk, wv, wo, gain_one, gain_two, table, router, expert_in, expert_out):
        first_norm_output = low(rms_scale(resid, gain_one))
        query = low_back(low(project(first_norm_output, wq)))
        key_all = low_back(low(project(first_norm_output, wk)))
        value_all = low_back(low(project(first_norm_output, wv)))
        band = dot_high(one_hot, table)
        bias = jnp.transpose(band[offsets], (2, 0, 1))

        def attend(parts):
            query_seq, key_sequence, value_seq = parts
            query_h = query_seq.reshape(LEN, HEADS, HEAD_DIM)
            key_h = key_sequence.reshape(LEN, HEADS, HEAD_DIM)
            value_h = value_seq.reshape(LEN, HEADS, HEAD_DIM)
            scores = jnp.einsum('qhd,khd->hqk', query_h, key_h, precision=lax.Precision.HIGHEST) + bias
            scores = low_back(scores)
            probs = low(jax.nn.softmax(scores, axis=-1))
            mixed = jnp.einsum('hqk,khd->qhd', probs, value_h, precision=lax.Precision.HIGHEST)
            return mixed.reshape(LEN, D)
        attention_result = lax.map(jax.checkpoint(attend), (query, key_all, value_all))
        attention_result = low_back(low(attention_result))
        middle = resid + low_back(project(attention_result, wo))
        norm_two = rms_scale(middle, gain_two)
        logits = project(norm_two, router)
        route_probs = jax.nn.softmax(logits, axis=-1)
        gate = lax.optimization_barrier(jnp.sum(route_probs * route_hot, axis=-1))
        sent = low_back(low(norm_two)).reshape(blocks, TOK_DEV, D)
        padded = jnp.concatenate([sent, jnp.zeros((blocks, 1, D), jnp.float32)], axis=1)
        buffer = jnp.take_along_axis(padded, slot_token[..., None], axis=1)
        per_expert = buffer.reshape(blocks, EXPERTS, CAP, D).transpose(1, 0, 2, 3).reshape(EXPERTS, blocks * CAP, D)

        def expert(parts):
            rows_in, weight_in, weight_out = parts
            pre_act = low_back(dot_high(rows_in, weight_in))
            act = low(jax.nn.gelu(pre_act))
            return low_back(low(dot_high(act, weight_out)))
        returned = lax.map(jax.checkpoint(expert), (per_expert, expert_in, expert_out))
        returned = returned.reshape(EXPERTS, blocks, CAP, D).transpose(1, 0, 2, 3).reshape(blocks, EXPERTS * CAP, D)
        routed = jnp.take_along_axis(returned, read_index[..., None], axis=1) * kept[..., None].astype(jnp.float32)
        return middle + gate[..., None] * routed.reshape(SEQS, LEN, D)
    inputs = (tokens.astype(jnp.float32), w_query.astype(jnp.float32), w_key.astype(jnp.float32), w_value.astype(jnp.float32), w_output.astype(jnp.float32), gain_attn, gain_ffn, bias_table, w_router, w_in.astype(jnp.float32), w_out.astype(jnp.float32))
    result, pullback = jax.vjp(forward, *inputs)
    grads = pullback(cotangent.astype(jnp.float32))
    return (result.astype(jnp.bfloat16), grads[0], grads[1], grads[2], grads[3], grads[4], grads[5], grads[6], grads[7], grads[8], grads[9], grads[10])
```

```python
import functools

import jax
import jax.numpy as jnp
from jax import lax
from jax.experimental import pallas as pl
from jax.experimental.pallas import tpu as pltpu
from jax.sharding import PartitionSpec as P

SINGLE = jnp.float32
BFLOAT = jnp.bfloat16
NT = (((1,), (1,)), ((), ()))
TN = (((0,), (0,)), ((), ()))


def rms_scale(value_rows, gain):
    return (
        value_rows
        * lax.rsqrt(jnp.mean(value_rows * value_rows, axis=-1, keepdims=True) + 1e-06)
        * gain
    )


def mm(left, right, dims=(((1,), (0,)), ((), ()))):
    return lax.dot_general(left, right, dims, preferred_element_type=SINGLE)


def lane_mask(shape, part, head_dim):
    return lax.broadcasted_iota(jnp.int32, shape, 1) // head_dim == part


def biased_scores(query, key, window_row):
    rows, cols = query.shape[0], key.shape[0]
    width = window_row.shape[1]
    spread = jnp.broadcast_to(window_row, (rows, width))
    shifted = pltpu.roll(spread, width - rows + 1, 1, stride=1, stride_axis=0)
    return mm(query, key, NT) + shifted[:, :cols]


def attend_kernel(head_dim, q_ref, k_ref, v_ref, win_ref, o_ref, lse_ref):
    query, key, value = q_ref[...], k_ref[...], v_ref[...]
    total = jnp.zeros(query.shape, SINGLE)
    for part in range(query.shape[1] // head_dim):
        mask = lane_mask(query.shape, part, head_dim)
        scores = biased_scores(jnp.where(mask, query, 0), key, win_ref[part])
        top = jnp.max(scores, axis=-1, keepdims=True)
        raised = jnp.exp(scores - top)
        summed = jnp.sum(raised, axis=-1, keepdims=True)
        lse_ref[part] = top + jnp.log(summed)
        probs = (raised * (1.0 / summed)).astype(BFLOAT)
        total = jnp.where(mask, mm(probs, value), total)
    o_ref[...] = total.astype(BFLOAT)


def attend_back_kernel(
    head_dim, q_ref, k_ref, v_ref, do_ref, lse_ref, win_ref, dq_ref, dkv_ref, diag_ref
):
    query, key, value, grad = q_ref[...], k_ref[...], v_ref[...], do_ref[...]
    rows, cols = query.shape[0], key.shape[0]
    blocks = cols // rows
    grad_q = jnp.zeros(query.shape, SINGLE)
    grad_k = jnp.zeros(key.shape, SINGLE)
    grad_v = jnp.zeros(key.shape, SINGLE)
    flip = (
        lax.broadcasted_iota(jnp.int32, (rows, rows), 0)
        + lax.broadcasted_iota(jnp.int32, (rows, rows), 1)
        == rows - 1
    ).astype(SINGLE).astype(BFLOAT)
    for part in range(query.shape[1] // head_dim):
        mask = lane_mask(query.shape, part, head_dim)
        mask_k = lane_mask(key.shape, part, head_dim)
        scores = biased_scores(jnp.where(mask, query, 0), key, win_ref[part])
        probs = jnp.exp(scores - lse_ref[part])
        grad_probs = mm(jnp.where(mask, grad, 0), value, NT)
        inner = jnp.sum(probs * grad_probs, axis=-1, keepdims=True)
        grad_scores = (probs * (grad_probs - inner)).astype(BFLOAT)
        grad_q = jnp.where(mask, mm(grad_scores, key), grad_q)
        grad_k = jnp.where(mask_k, mm(grad_scores, query, TN), grad_k)
        grad_v = jnp.where(mask_k, mm(probs.astype(BFLOAT), grad, TN), grad_v)
        turned = jnp.concatenate(
            [mm(flip, grad_scores), jnp.zeros((rows, rows), SINGLE)], axis=1
        )
        lined = pltpu.roll(turned, 0, 1, stride=1, stride_axis=0)
        diag_ref[part] = jnp.sum(lined, axis=0, keepdims=True)
    dq_ref[...] = grad_q.astype(BFLOAT)
    grad_k, grad_v = grad_k.astype(BFLOAT), grad_v.astype(BFLOAT)
    for block in range(blocks):
        dkv_ref[block, 0] = grad_k[block * rows : (block + 1) * rows]
        dkv_ref[block, 1] = grad_v[block * rows : (block + 1) * rows]


def attention_specs(rows, cols, lanes, parts, pairs, span):
    return dict(
        q=pl.BlockSpec((rows, lanes), lambda p: (0, p)),
        k=pl.BlockSpec((cols, lanes), lambda p: (0, p)),
        v=pl.BlockSpec((cols, lanes), lambda p: (0, p + pairs)),
        win=pl.BlockSpec((parts, 1, span), lambda p: (p, 0, 0)),
        lse=pl.BlockSpec((parts, rows, 1), lambda p: (p, 0, 0)),
    )


def attend(query, pair_all, window, head_dim):
    rows, width = query.shape
    cols, heads, span = pair_all.shape[0], window.shape[0], window.shape[2]
    lanes = max(128, head_dim)
    pairs, parts = width // lanes, lanes // head_dim
    spec = attention_specs(rows, cols, lanes, parts, pairs, span)
    return pl.pallas_call(
        functools.partial(attend_kernel, head_dim),
        grid=(pairs,),
        in_specs=[spec["q"], spec["k"], spec["v"], spec["win"]],
        out_specs=[spec["q"], spec["lse"]],
        out_shape=[
            jax.ShapeDtypeStruct((rows, width), BFLOAT),
            jax.ShapeDtypeStruct((heads, rows, 1), SINGLE),
        ],
        compiler_params=pltpu.CompilerParams(vmem_limit_bytes=40 * 2**20),
        cost_estimate=pl.CostEstimate(
            flops=4 * rows * cols * width,
            bytes_accessed=4 * cols * width + 4 * rows * width,
            transcendentals=heads * rows * cols,
        ),
    )(query, pair_all, pair_all, window)


def attend_back(query, pair_all, grad, lse, window, head_dim):
    rows, width = query.shape
    cols, heads, span = pair_all.shape[0], window.shape[0], window.shape[2]
    lanes = max(128, head_dim)
    pairs, parts = width // lanes, lanes // head_dim
    spec = attention_specs(rows, cols, lanes, parts, pairs, span)
    blocks = cols // rows
    return pl.pallas_call(
        functools.partial(attend_back_kernel, head_dim),
        grid=(pairs,),
        in_specs=[spec["q"], spec["k"], spec["v"], spec["q"], spec["lse"], spec["win"]],
        out_specs=[
            spec["q"],
            pl.BlockSpec((blocks, 2, rows, lanes), lambda p: (0, 0, 0, p)),
            spec["win"],
        ],
        out_shape=[
            jax.ShapeDtypeStruct((rows, width), BFLOAT),
            jax.ShapeDtypeStruct((blocks, 2, rows, width), BFLOAT),
            jax.ShapeDtypeStruct((heads, 1, span), SINGLE),
        ],
        compiler_params=pltpu.CompilerParams(vmem_limit_bytes=48 * 2**20),
        cost_estimate=pl.CostEstimate(
            flops=12 * rows * cols * width,
            bytes_accessed=8 * cols * width + 8 * rows * width,
            transcendentals=heads * rows * cols,
        ),
    )(query, pair_all, pair_all, grad, lse, window)


def weight_kernel(rows_ref, pre_ref, act_ref, grad_ref, in_ref, out_ref):
    in_ref[0, 0] = mm(rows_ref[0], pre_ref[0], TN).astype(BFLOAT)
    out_ref[0, 0] = mm(act_ref[0], grad_ref[0], TN).astype(BFLOAT)


def weight_grads(rows, grad_pre, act, grad, shares):
    experts, count, width = rows.shape
    hidden = act.shape[2]
    share = hidden // shares
    whole = pl.BlockSpec((1, count, width), lambda e, s: (e, 0, 0))
    part = pl.BlockSpec((1, count, share), lambda e, s: (e, 0, s))
    return pl.pallas_call(
        weight_kernel,
        grid=(experts, shares),
        in_specs=[whole, part, part, whole],
        out_specs=[
            pl.BlockSpec((1, 1, width, share), lambda e, s: (s, e, 0, 0)),
            pl.BlockSpec((1, 1, share, width), lambda e, s: (s, e, 0, 0)),
        ],
        out_shape=[
            jax.ShapeDtypeStruct((shares, experts, width, share), BFLOAT),
            jax.ShapeDtypeStruct((shares, experts, share, width), BFLOAT),
        ],
        compiler_params=pltpu.CompilerParams(vmem_limit_bytes=32 * 2**20),
        cost_estimate=pl.CostEstimate(
            flops=4 * experts * count * width * hidden,
            bytes_accessed=4 * experts * width * hidden,
            transcendentals=0,
        ),
    )(rows, grad_pre, act, grad)


def on_device(
    tokens,
    cotangent,
    w_query,
    w_key,
    w_value,
    w_output,
    gain_attn,
    gain_ffn,
    bias_table,
    w_router,
    w_in,
    w_out,
    routes,
    slots,
    buckets,
):
    tok_count = tokens.shape[1]
    width = tokens.shape[2]
    heads = bias_table.shape[1]
    bucket_count = bias_table.shape[0]
    head_dim = width // heads
    n_context = lax.axis_size("context")
    seq_len = tok_count * n_context
    n_owner = lax.axis_size("experts")
    shares = n_context * lax.axis_size("dp")
    expert_dev = w_in.shape[0]
    capacity = 2 * tok_count // (expert_dev * n_owner)
    highest = lax.Precision.HIGHEST
    resid = tokens[0].astype(SINGLE)
    first_norm_output = rms_scale(resid, gain_attn).astype(BFLOAT)
    pair_bf = jnp.concatenate(
        [mm(first_norm_output, w_key).astype(BFLOAT), mm(first_norm_output, w_value).astype(BFLOAT)],
        axis=1,
    )
    pair_all = lax.all_gather(pair_bf, "context", axis=0, tiled=True)
    query_bf = mm(first_norm_output, w_query).astype(BFLOAT)
    span = seq_len + tok_count
    first = seq_len - (lax.axis_index("context") + 1) * tok_count
    bucket_window = lax.dynamic_slice(jnp.pad(buckets, (0, 1)), (first,), (span,))
    window_hot = (
        bucket_window[:, None] == jnp.arange(bucket_count, dtype=jnp.int32)[None, :]
    ).astype(SINGLE)
    window = jnp.einsum("ob,bh->ho", window_hot, bias_table, precision=highest)[:, None, :]
    attention_result, log_total = attend(query_bf, pair_all, window, head_dim)
    residual_middle = resid + mm(attention_result, w_output)
    norm_two = rms_scale(residual_middle, gain_ffn)
    logits = jnp.dot(norm_two, w_router, precision=highest)
    route_probs = jax.nn.softmax(logits, axis=-1)
    route_row = routes[0]
    slot_row = slots[0]
    route_hot = (
        route_row[:, None] == jnp.arange(logits.shape[1], dtype=jnp.int32)[None, :]
    ).astype(SINGLE)
    gate = jnp.sum(route_probs * route_hot, axis=-1)
    grad_out = cotangent[0].astype(SINGLE)
    grad_routed = (grad_out * gate[:, None]).astype(BFLOAT)
    slot_count = expert_dev * n_owner * capacity
    layout = (
        route_row // expert_dev * (expert_dev * capacity)
        + route_row % expert_dev * capacity
        + slot_row
    )
    place = jnp.where(slot_row < capacity, layout, -1)
    slot_hot = (place[:, None] == jnp.arange(slot_count, dtype=jnp.int32)[None, :]).astype(BFLOAT)
    send = mm(
        slot_hot, jnp.concatenate([norm_two.astype(BFLOAT), grad_routed], axis=1), TN
    ).astype(BFLOAT)
    arrived = lax.all_to_all(
        send.reshape(n_owner, expert_dev, capacity, 2 * width),
        "experts", split_axis=0, concat_axis=0, tiled=True,
    )
    arrived = arrived.transpose(1, 0, 2, 3).reshape(expert_dev, n_owner * capacity, 2 * width)
    rows, grad_expert = arrived[:, :, :width], arrived[:, :, width:]
    pre_act = jnp.einsum("erd,edf->erf", rows, w_in, preferred_element_type=SINGLE)
    act_bf = jax.nn.gelu(pre_act).astype(BFLOAT)
    expert_back = jnp.einsum("erf,efd->erd", act_bf, w_out, preferred_element_type=SINGLE).astype(
        BFLOAT
    )
    grad_act = jnp.einsum("erd,efd->erf", grad_expert, w_out, preferred_element_type=SINGLE)
    grad_pre = jax.vjp(jax.nn.gelu, pre_act)[1](grad_act)[0].astype(BFLOAT)
    grad_rows = jnp.einsum("erf,edf->erd", grad_pre, w_in, preferred_element_type=SINGLE).astype(
        BFLOAT
    )
    both_back = jnp.concatenate([expert_back, grad_rows], axis=2)
    both_back = both_back.reshape(expert_dev, n_owner, capacity, 2 * width).transpose(1, 0, 2, 3)
    returned = lax.all_to_all(
        both_back, "experts", split_axis=0, concat_axis=0, tiled=True
    ).reshape(slot_count, 2 * width)
    whole_in, whole_out = weight_grads(rows, grad_pre, act_bf, grad_expert, shares)
    grad_w_in = lax.psum_scatter(whole_in, ("context", "dp"), scatter_dimension=0, tiled=True)
    grad_w_out = lax.psum_scatter(whole_out, ("context", "dp"), scatter_dimension=0, tiled=True)
    fetched = mm(slot_hot, returned)
    routed = fetched[:, :width]
    output = residual_middle + gate[:, None] * routed
    grad_gate = jnp.sum(grad_out * routed, axis=-1)
    grad_logits = grad_gate[:, None] * route_probs * (route_hot - gate[:, None])
    grad_router = jnp.einsum("td,te->de", norm_two, grad_logits, precision=highest)
    grad_norm_two = fetched[:, width:] + jnp.einsum(
        "te,de->td", grad_logits, w_router, precision=highest
    )
    grad_mid, grad_gain_ffn = jax.vjp(rms_scale, residual_middle, gain_ffn)[1](grad_norm_two)
    grad_mid = grad_mid + grad_out
    grad_attn = grad_mid.astype(BFLOAT)
    grad_output = mm(attention_result, grad_attn, TN)
    grad_attended = mm(grad_attn, w_output, NT).astype(BFLOAT)
    grad_q, grad_pair, diagonal = attend_back(
        query_bf, pair_all, grad_attended, log_total, window, head_dim
    )
    grad_pair = lax.psum_scatter(grad_pair, "context", scatter_dimension=0, tiled=True)[0]
    grad_k, grad_v = grad_pair[0], grad_pair[1]
    grad_table = jnp.einsum("ho,ob->bh", diagonal[:, 0, :], window_hot, precision=highest)
    grad_query = mm(first_norm_output, grad_q, TN)
    grad_key = mm(first_norm_output, grad_k, TN)
    grad_value = mm(first_norm_output, grad_v, TN)
    grad_norm_one = mm(grad_q, w_query, NT) + mm(grad_k, w_key, NT) + mm(grad_v, w_value, NT)
    grad_resid, grad_gain_attn = jax.vjp(rms_scale, resid, gain_attn)[1](grad_norm_one)
    grad_tokens = grad_resid + grad_mid
    grads = (
        grad_query,
        grad_key,
        grad_value,
        grad_output,
        grad_gain_attn,
        grad_gain_ffn,
        grad_table,
        grad_router,
    )
    small = jnp.concatenate([grad.reshape(-1) for grad in grads[4:]])
    small_rows = -(-small.shape[0] // width // 16) * 16
    small = jnp.pad(small, (0, small_rows * width - small.shape[0])).reshape(small_rows, width)
    packed = jnp.concatenate([*grads[:4], small], axis=0).astype(BFLOAT)
    packed = lax.psum(packed, ("experts", "context", "dp")).astype(SINGLE)
    summed = [packed[at * width : (at + 1) * width] for at in range(4)]
    flat, at = packed[4 * width :].reshape(-1), 0
    for grad in grads[4:]:
        summed.append(flat[at : at + grad.size].reshape(grad.shape))
        at += grad.size
    return (
        output.astype(BFLOAT)[None],
        grad_tokens[None],
        summed[0],
        summed[1],
        summed[2],
        summed[3],
        summed[4],
        summed[5],
        summed[6],
        summed[7],
        grad_w_in[0].astype(SINGLE),
        grad_w_out[0].astype(SINGLE),
    )


def solution(mesh):
    in_specs = (
        P(("experts", "dp"), "context", None),
        P(("experts", "dp"), "context", None),
        P(),
        P(),
        P(),
        P(),
        P(),
        P(),
        P(),
        P(),
        P("experts", None, None),
        P("experts", None, None),
        P(("experts", "dp"), "context"),
        P(("experts", "dp"), "context"),
        P(),
    )
    out_specs = (
        P(("experts", "dp"), "context", None),
        P(("experts", "dp"), "context", None),
        P(),
        P(),
        P(),
        P(),
        P(),
        P(),
        P(),
        P(),
        P("experts", None, ("context", "dp")),
        P("experts", ("context", "dp"), None),
    )
    return jax.shard_map(
        on_device, mesh=mesh, in_specs=in_specs, out_specs=out_specs, check_vma=False
    )
```

```python
import functools

import jax
import jax.numpy as jnp
from jax import lax
from jax.experimental import pallas as pl
from jax.experimental.pallas import tpu as pltpu
from jax.sharding import PartitionSpec as P

SINGLE = jnp.float32
BFLOAT = jnp.bfloat16
NT = (((1,), (1,)), ((), ()))
TN = (((0,), (0,)), ((), ()))


def rms_scale(value_rows, gain):
    return (
        value_rows
        * lax.rsqrt(jnp.mean(value_rows * value_rows, axis=-1, keepdims=True) + 1e-06)
        * gain
    )


def mm(left, right, dims=(((1,), (0,)), ((), ()))):
    return lax.dot_general(left, right, dims, preferred_element_type=SINGLE)


def lane_mask(shape, part, head_dim):
    return lax.broadcasted_iota(jnp.int32, shape, 1) // head_dim == part


def biased_scores(query, key, window_row):
    rows, cols = query.shape[0], key.shape[0]
    width = window_row.shape[1]
    spread = jnp.broadcast_to(window_row, (rows, width))
    shifted = pltpu.roll(spread, width - rows + 1, 1, stride=1, stride_axis=0)
    return mm(query, key, NT) + shifted[:, :cols]


def attend_kernel(head_dim, q_ref, k_ref, v_ref, win_ref, o_ref, lse_ref):
    query, key, value = q_ref[...], k_ref[...], v_ref[...]
    total = jnp.zeros(query.shape, SINGLE)
    for part in range(query.shape[1] // head_dim):
        mask = lane_mask(query.shape, part, head_dim)
        scores = biased_scores(jnp.where(mask, query, 0), key, win_ref[part])
        top = jnp.max(scores, axis=-1, keepdims=True)
        raised = jnp.exp(scores - top)
        summed = jnp.sum(raised, axis=-1, keepdims=True)
        lse_ref[part] = top + jnp.log(summed)
        probs = (raised * (1.0 / summed)).astype(BFLOAT)
        total = jnp.where(mask, mm(probs, value), total)
    o_ref[...] = total.astype(BFLOAT)


def attend_back_kernel(
    head_dim, q_ref, k_ref, v_ref, do_ref, lse_ref, win_ref, dq_ref, dkv_ref, diag_ref
):
    query, key, value, grad = q_ref[...], k_ref[...], v_ref[...], do_ref[...]
    rows, cols = query.shape[0], key.shape[0]
    blocks = cols // rows
    grad_q = jnp.zeros(query.shape, SINGLE)
    grad_k = jnp.zeros(key.shape, SINGLE)
    grad_v = jnp.zeros(key.shape, SINGLE)
    flip = (
        lax.broadcasted_iota(jnp.int32, (rows, rows), 0)
        + lax.broadcasted_iota(jnp.int32, (rows, rows), 1)
        == rows - 1
    ).astype(SINGLE).astype(BFLOAT)
    for part in range(query.shape[1] // head_dim):
        mask = lane_mask(query.shape, part, head_dim)
        mask_k = lane_mask(key.shape, part, head_dim)
        scores = biased_scores(jnp.where(mask, query, 0), key, win_ref[part])
        probs = jnp.exp(scores - lse_ref[part])
        grad_probs = mm(jnp.where(mask, grad, 0), value, NT)
        inner = jnp.sum(probs * grad_probs, axis=-1, keepdims=True)
        grad_scores = (probs * (grad_probs - inner)).astype(BFLOAT)
        grad_q = jnp.where(mask, mm(grad_scores, key), grad_q)
        grad_k = jnp.where(mask_k, mm(grad_scores, query, TN), grad_k)
        grad_v = jnp.where(mask_k, mm(probs.astype(BFLOAT), grad, TN), grad_v)
        turned = jnp.concatenate(
            [mm(flip, grad_scores), jnp.zeros((rows, rows), SINGLE)], axis=1
        )
        lined = pltpu.roll(turned, 0, 1, stride=1, stride_axis=0)
        diag_ref[part] = jnp.sum(lined, axis=0, keepdims=True)
    dq_ref[...] = grad_q.astype(BFLOAT)
    grad_k, grad_v = grad_k.astype(BFLOAT), grad_v.astype(BFLOAT)
    for block in range(blocks):
        dkv_ref[block, 0] = grad_k[block * rows : (block + 1) * rows]
        dkv_ref[block, 1] = grad_v[block * rows : (block + 1) * rows]


def attention_specs(rows, cols, lanes, parts, pairs, span):
    return dict(
        q=pl.BlockSpec((rows, lanes), lambda p: (0, p)),
        k=pl.BlockSpec((cols, lanes), lambda p: (0, p)),
        v=pl.BlockSpec((cols, lanes), lambda p: (0, p + pairs)),
        win=pl.BlockSpec((parts, 1, span), lambda p: (p, 0, 0)),
        lse=pl.BlockSpec((parts, rows, 1), lambda p: (p, 0, 0)),
    )


def attend(query, pair_all, window, head_dim):
    rows, width = query.shape
    cols, heads, span = pair_all.shape[0], window.shape[0], window.shape[2]
    lanes = max(128, head_dim)
    pairs, parts = width // lanes, lanes // head_dim
    spec = attention_specs(rows, cols, lanes, parts, pairs, span)
    return pl.pallas_call(
        functools.partial(attend_kernel, head_dim),
        grid=(pairs,),
        in_specs=[spec["q"], spec["k"], spec["v"], spec["win"]],
        out_specs=[spec["q"], spec["lse"]],
        out_shape=[
            jax.ShapeDtypeStruct((rows, width), BFLOAT),
            jax.ShapeDtypeStruct((heads, rows, 1), SINGLE),
        ],
        compiler_params=pltpu.CompilerParams(vmem_limit_bytes=40 * 2**20),
        cost_estimate=pl.CostEstimate(
            flops=4 * rows * cols * width,
            bytes_accessed=4 * cols * width + 4 * rows * width,
            transcendentals=heads * rows * cols,
        ),
    )(query, pair_all, pair_all, window)


def attend_back(query, pair_all, grad, lse, window, head_dim):
    rows, width = query.shape
    cols, heads, span = pair_all.shape[0], window.shape[0], window.shape[2]
    lanes = max(128, head_dim)
    pairs, parts = width // lanes, lanes // head_dim
    spec = attention_specs(rows, cols, lanes, parts, pairs, span)
    blocks = cols // rows
    return pl.pallas_call(
        functools.partial(attend_back_kernel, head_dim),
        grid=(pairs,),
        in_specs=[spec["q"], spec["k"], spec["v"], spec["q"], spec["lse"], spec["win"]],
        out_specs=[
            spec["q"],
            pl.BlockSpec((blocks, 2, rows, lanes), lambda p: (0, 0, 0, p)),
            spec["win"],
        ],
        out_shape=[
            jax.ShapeDtypeStruct((rows, width), BFLOAT),
            jax.ShapeDtypeStruct((blocks, 2, rows, width), BFLOAT),
            jax.ShapeDtypeStruct((heads, 1, span), SINGLE),
        ],
        compiler_params=pltpu.CompilerParams(vmem_limit_bytes=48 * 2**20),
        cost_estimate=pl.CostEstimate(
            flops=12 * rows * cols * width,
            bytes_accessed=8 * cols * width + 8 * rows * width,
            transcendentals=heads * rows * cols,
        ),
    )(query, pair_all, pair_all, grad, lse, window)


def weight_kernel(rows_ref, pre_ref, act_ref, grad_ref, in_ref, out_ref):
    in_ref[0, 0] = mm(rows_ref[0], pre_ref[0], TN).astype(BFLOAT)
    out_ref[0, 0] = mm(act_ref[0], grad_ref[0], TN).astype(BFLOAT)


def weight_grads(rows, grad_pre, act, grad, shares):
    experts, count, width = rows.shape
    hidden = act.shape[2]
    share = hidden // shares
    whole = pl.BlockSpec((1, count, width), lambda e, s: (e, 0, 0))
    part = pl.BlockSpec((1, count, share), lambda e, s: (e, 0, s))
    return pl.pallas_call(
        weight_kernel,
        grid=(experts, shares),
        in_specs=[whole, part, part, whole],
        out_specs=[
            pl.BlockSpec((1, 1, width, share), lambda e, s: (s, e, 0, 0)),
            pl.BlockSpec((1, 1, share, width), lambda e, s: (s, e, 0, 0)),
        ],
        out_shape=[
            jax.ShapeDtypeStruct((shares, experts, width, share), BFLOAT),
            jax.ShapeDtypeStruct((shares, experts, share, width), BFLOAT),
        ],
        compiler_params=pltpu.CompilerParams(vmem_limit_bytes=32 * 2**20),
        cost_estimate=pl.CostEstimate(
            flops=4 * experts * count * width * hidden,
            bytes_accessed=4 * experts * width * hidden,
            transcendentals=0,
        ),
    )(rows, grad_pre, act, grad)


MESH = pl.DeviceIdType.MESH
ANY = pl.BlockSpec(memory_space=pl.ANY)
VMEM = pl.BlockSpec(memory_space=pltpu.VMEM)


def greet(peers):
    barrier = pltpu.get_barrier_semaphore()
    for peer in peers:
        pl.semaphore_signal(barrier, inc=1, device_id=peer, device_id_type=MESH)
    pl.semaphore_wait(barrier, len(peers))


def remote(src, dst, send_sem, recv_sem, peer):
    copy = pltpu.make_async_remote_copy(
        src_ref=src,
        dst_ref=dst,
        send_sem=send_sem,
        recv_sem=recv_sem,
        device_id=peer,
        device_id_type=MESH,
    )
    copy.start()
    return copy


def add_tiles(rows, own, others, store):
    tile = 64 if rows % 64 == 0 else rows

    def add(step, carry):
        at = pl.ds(pl.multiple_of(step * tile, tile), tile)
        total = own(step * tile, tile)
        for other in others:
            total = total + other[at].astype(SINGLE)
        store(step * tile, tile, total)
        return carry

    lax.fori_loop(0, rows // tile, add, 0)


def swap_kernel(axis, count, gather, x_ref, o_ref, send_sem, recv_sem, own_sem):
    me = lax.axis_index(axis)
    peers = [lax.rem(me + step, count) for step in range(1, count)]
    greet([{axis: peer} for peer in peers])
    copies = [
        remote(
            x_ref if gather else x_ref.at[peer],
            o_ref.at[me],
            send_sem.at[at],
            recv_sem.at[at],
            {axis: peer},
        )
        for at, peer in enumerate(peers)
    ]
    own = pltpu.make_async_copy(x_ref if gather else x_ref.at[me], o_ref.at[me], own_sem)
    own.start()
    own.wait()
    for copy in copies:
        copy.wait()


def swap(x, axis, collective_id, gather=False):
    count = lax.axis_size(axis)
    shape = (count, *x.shape) if gather else x.shape
    return pl.pallas_call(
        functools.partial(swap_kernel, axis, count, gather),
        in_specs=[ANY],
        out_specs=ANY,
        out_shape=jax.ShapeDtypeStruct(shape, x.dtype),
        scratch_shapes=[
            pltpu.SemaphoreType.DMA((count - 1,)),
            pltpu.SemaphoreType.DMA((count - 1,)),
            pltpu.SemaphoreType.DMA,
        ],
        compiler_params=pltpu.CompilerParams(collective_id=collective_id, has_side_effects=True),
    )(x)


def sum_kernel(axis, count, x_ref, o_ref, own, held, send_sem, recv_sem, own_sem):
    me = lax.axis_index(axis)
    peers = [lax.rem(me + step, count) for step in range(1, count)]
    greet([{axis: peer} for peer in peers])
    copies = [
        remote(x_ref.at[peer], held.at[at], send_sem.at[at], recv_sem.at[at], {axis: peer})
        for at, peer in enumerate(peers)
    ]
    mine = pltpu.make_async_copy(x_ref.at[me], own, own_sem)
    mine.start()
    mine.wait()
    for copy in copies:
        copy.wait()

    def load(at, tile):
        return own[pl.ds(pl.multiple_of(at, tile), tile)].astype(SINGLE)

    def store(at, tile, total):
        o_ref[pl.ds(pl.multiple_of(at, tile), tile)] = total.astype(BFLOAT)

    add_tiles(own.shape[0], load, [held.at[at] for at in range(count - 1)], store)


def sum_shares(x, axis, collective_id):
    count, rows, width = x.shape
    return pl.pallas_call(
        functools.partial(sum_kernel, axis, count),
        in_specs=[ANY],
        out_specs=VMEM,
        out_shape=jax.ShapeDtypeStruct((rows, width), x.dtype),
        scratch_shapes=[
            pltpu.VMEM((rows, width), x.dtype),
            pltpu.VMEM((count - 1, rows, width), x.dtype),
            pltpu.SemaphoreType.DMA((count - 1,)),
            pltpu.SemaphoreType.DMA((count - 1,)),
            pltpu.SemaphoreType.DMA,
        ],
        compiler_params=pltpu.CompilerParams(
            collective_id=collective_id, has_side_effects=True, vmem_limit_bytes=24 * 2**20
        ),
    )(x)


def reduce_kernel(orders, sizes, *refs):
    count = len(orders)
    x_refs, o_refs, scratch = refs[:count], refs[count : 2 * count], refs[2 * count :]
    send_sem, recv_sem = scratch[-2:]
    me = {axis: lax.axis_index(axis) for axis in sizes}
    peers = {
        axis: [lax.rem(me[axis] + step, size) for step in range(1, size)]
        for axis, size in sizes.items()
    }
    greet([{axis: peer} for axis in sizes for peer in peers[axis]])
    depth = len(sizes)
    held = [scratch[2 * depth * at : 2 * depth * at + depth] for at in range(count)]
    part = [scratch[2 * depth * at + depth : 2 * depth * (at + 1)] for at in range(count)]
    chunks, places = [], []
    for at, order in enumerate(orders):
        rows, place, own_chunks, own_places = x_refs[at].shape[0], 0, [], []
        for axis in order:
            rows = rows // sizes[axis]
            place = place + me[axis] * rows
            own_chunks.append(rows)
            own_places.append(place)
        chunks.append(own_chunks)
        places.append(own_places)

    def begin(at, phase):
        level = phase if phase < depth else 2 * depth - 1 - phase
        axis, chunk = orders[at][level], chunks[at][level]
        copies = []
        for slot, peer in enumerate(peers[axis]):
            if phase < depth:
                source = x_refs[at] if level == 0 else part[at][level - 1]
                src = source.at[pl.ds(pl.multiple_of(peer * chunk, chunk), chunk)]
                dst = held[at][level].at[slot]
            else:
                where = pl.ds(pl.multiple_of(places[at][level], chunk), chunk)
                src = dst = o_refs[at].at[where]
            sems = send_sem.at[at, phase, slot], recv_sem.at[at, phase, slot]
            copies.append(remote(src, dst, *sems, {axis: peer}))
        return copies

    def finish(at, phase, copies):
        for copy in copies:
            copy.wait()
        if phase >= depth:
            return
        axis, chunk = orders[at][phase], chunks[at][phase]
        source = x_refs[at] if phase == 0 else part[at][phase - 1]
        last = phase == depth - 1
        target = o_refs[at] if last else part[at][phase]
        base = pl.multiple_of(places[at][phase], chunk) if last else 0
        start = me[axis] * chunk

        def load(row, tile):
            return source[pl.ds(pl.multiple_of(start + row, tile), tile)].astype(SINGLE)

        def store(row, tile, total):
            target[pl.ds(pl.multiple_of(base + row, tile), tile)] = total.astype(target.dtype)

        add_tiles(chunk, load, [held[at][phase].at[slot] for slot in range(len(peers[axis]))], store)

    flying = [None] * count
    for phase in range(2 * depth + 1):
        for at in range(count):
            if phase > 0:
                finish(at, phase - 1, flying[at])
            if phase < 2 * depth:
                flying[at] = begin(at, phase)


def reduce_all(pieces, orders, collective_id):
    sizes = {axis: lax.axis_size(axis) for axis in orders[0]}
    scratch = []
    for piece, order in zip(pieces, orders):
        rows, width = piece.shape
        held, part = [], []
        for axis in order:
            rows = rows // sizes[axis]
            held.append(pltpu.VMEM((sizes[axis] - 1, rows, width), piece.dtype))
            part.append(pltpu.VMEM((rows, width), piece.dtype))
        scratch += held + part
    sems = (len(pieces), 2 * len(sizes), max(sizes.values()) - 1)
    return pl.pallas_call(
        functools.partial(reduce_kernel, orders, sizes),
        in_specs=[VMEM] * len(pieces),
        out_specs=[VMEM] * len(pieces),
        out_shape=[jax.ShapeDtypeStruct(piece.shape, piece.dtype) for piece in pieces],
        scratch_shapes=scratch + [pltpu.SemaphoreType.DMA(sems), pltpu.SemaphoreType.DMA(sems)],
        compiler_params=pltpu.CompilerParams(
            collective_id=collective_id, has_side_effects=True, vmem_limit_bytes=48 * 2**20
        ),
    )(*pieces)


def on_device(
    tokens,
    cotangent,
    w_query,
    w_key,
    w_value,
    w_output,
    gain_attn,
    gain_ffn,
    bias_table,
    w_router,
    w_in,
    w_out,
    routes,
    slots,
    buckets,
):
    tok_count = tokens.shape[1]
    width = tokens.shape[2]
    heads = bias_table.shape[1]
    bucket_count = bias_table.shape[0]
    head_dim = width // heads
    n_context = lax.axis_size("context")
    seq_len = tok_count * n_context
    n_owner = lax.axis_size("experts")
    shares = n_context * lax.axis_size("dp")
    expert_dev = w_in.shape[0]
    capacity = 2 * tok_count // (expert_dev * n_owner)
    highest = lax.Precision.HIGHEST
    resid = tokens[0].astype(SINGLE)
    first_norm_output = rms_scale(resid, gain_attn).astype(BFLOAT)
    pair_bf = jnp.concatenate(
        [mm(first_norm_output, w_key).astype(BFLOAT), mm(first_norm_output, w_value).astype(BFLOAT)],
        axis=1,
    )
    pair_all = swap(pair_bf, "context", 0, gather=True).reshape(seq_len, 2 * width)
    query_bf = mm(first_norm_output, w_query).astype(BFLOAT)
    span = seq_len + tok_count
    first = seq_len - (lax.axis_index("context") + 1) * tok_count
    bucket_window = lax.dynamic_slice(jnp.pad(buckets, (0, 1)), (first,), (span,))
    window_hot = (
        bucket_window[:, None] == jnp.arange(bucket_count, dtype=jnp.int32)[None, :]
    ).astype(SINGLE)
    window = jnp.einsum("ob,bh->ho", window_hot, bias_table, precision=highest)[:, None, :]
    attention_result, log_total = attend(query_bf, pair_all, window, head_dim)
    residual_middle = resid + mm(attention_result, w_output)
    norm_two = rms_scale(residual_middle, gain_ffn)
    logits = jnp.dot(norm_two, w_router, precision=highest)
    route_probs = jax.nn.softmax(logits, axis=-1)
    route_row = routes[0]
    slot_row = slots[0]
    route_hot = (
        route_row[:, None] == jnp.arange(logits.shape[1], dtype=jnp.int32)[None, :]
    ).astype(SINGLE)
    gate = jnp.sum(route_probs * route_hot, axis=-1)
    grad_out = cotangent[0].astype(SINGLE)
    grad_routed = (grad_out * gate[:, None]).astype(BFLOAT)
    slot_count = expert_dev * n_owner * capacity
    layout = (
        route_row // expert_dev * (expert_dev * capacity)
        + route_row % expert_dev * capacity
        + slot_row
    )
    place = jnp.where(slot_row < capacity, layout, -1)
    slot_hot = (place[:, None] == jnp.arange(slot_count, dtype=jnp.int32)[None, :]).astype(BFLOAT)
    send = mm(
        slot_hot, jnp.concatenate([norm_two.astype(BFLOAT), grad_routed], axis=1), TN
    ).astype(BFLOAT)
    arrived = swap(send.reshape(n_owner, expert_dev * capacity, 2 * width), "experts", 1)
    arrived = arrived.reshape(n_owner, expert_dev, capacity, 2 * width)
    arrived = arrived.transpose(1, 0, 2, 3).reshape(expert_dev, n_owner * capacity, 2 * width)
    rows, grad_expert = arrived[:, :, :width], arrived[:, :, width:]
    pre_act = jnp.einsum("erd,edf->erf", rows, w_in, preferred_element_type=SINGLE)
    act_bf = jax.nn.gelu(pre_act).astype(BFLOAT)
    expert_back = jnp.einsum("erf,efd->erd", act_bf, w_out, preferred_element_type=SINGLE).astype(
        BFLOAT
    )
    grad_act = jnp.einsum("erd,efd->erf", grad_expert, w_out, preferred_element_type=SINGLE)
    grad_pre = jax.vjp(jax.nn.gelu, pre_act)[1](grad_act)[0].astype(BFLOAT)
    grad_rows = jnp.einsum("erf,edf->erd", grad_pre, w_in, preferred_element_type=SINGLE).astype(
        BFLOAT
    )
    both_back = jnp.concatenate([expert_back, grad_rows], axis=2)
    both_back = both_back.reshape(expert_dev, n_owner, capacity, 2 * width).transpose(1, 0, 2, 3)
    whole_in, whole_out = weight_grads(rows, grad_pre, act_bf, grad_expert, shares)
    both_back, whole_in, whole_out = lax.optimization_barrier((both_back, whole_in, whole_out))
    returned = swap(
        both_back.reshape(n_owner, expert_dev * capacity, 2 * width), "experts", 2
    ).reshape(slot_count, 2 * width)
    grad_w_in = lax.psum_scatter(whole_in, ("context", "dp"), scatter_dimension=0, tiled=True)
    grad_w_out = lax.psum_scatter(whole_out, ("context", "dp"), scatter_dimension=0, tiled=True)
    fetched = mm(slot_hot, returned)
    routed = fetched[:, :width]
    output = residual_middle + gate[:, None] * routed
    grad_gate = jnp.sum(grad_out * routed, axis=-1)
    grad_logits = grad_gate[:, None] * route_probs * (route_hot - gate[:, None])
    grad_router = jnp.einsum("td,te->de", norm_two, grad_logits, precision=highest)
    grad_norm_two = fetched[:, width:] + jnp.einsum(
        "te,de->td", grad_logits, w_router, precision=highest
    )
    grad_mid, grad_gain_ffn = jax.vjp(rms_scale, residual_middle, gain_ffn)[1](grad_norm_two)
    grad_mid = grad_mid + grad_out
    grad_attn = grad_mid.astype(BFLOAT)
    grad_output = mm(attention_result, grad_attn, TN)
    grad_attended = mm(grad_attn, w_output, NT).astype(BFLOAT)
    grad_q, grad_pair, diagonal = attend_back(
        query_bf, pair_all, grad_attended, log_total, window, head_dim
    )
    grad_pair = sum_shares(grad_pair.reshape(n_context, 2 * tok_count, width), "context", 3)
    grad_k, grad_v = grad_pair[:tok_count], grad_pair[tok_count:]
    grad_table = jnp.einsum("ho,ob->bh", diagonal[:, 0, :], window_hot, precision=highest)
    grad_query = mm(first_norm_output, grad_q, TN)
    grad_key = mm(first_norm_output, grad_k, TN)
    grad_value = mm(first_norm_output, grad_v, TN)
    grad_norm_one = mm(grad_q, w_query, NT) + mm(grad_k, w_key, NT) + mm(grad_v, w_value, NT)
    grad_resid, grad_gain_attn = jax.vjp(rms_scale, resid, gain_attn)[1](grad_norm_one)
    grad_tokens = grad_resid + grad_mid
    grads = (
        grad_query,
        grad_key,
        grad_value,
        grad_output,
        grad_gain_attn,
        grad_gain_ffn,
        grad_table,
        grad_router,
    )
    n_all = n_owner * shares
    small = jnp.concatenate([grad.reshape(-1) for grad in grads[4:]])
    small_rows = -(-small.shape[0] // (128 * 8 * n_all)) * 8 * n_all
    small = jnp.pad(small, (0, small_rows * 128 - small.shape[0])).reshape(small_rows, 128)
    unit = 16 * n_all
    units = -(-4 * width // unit)
    cut = -(-2 * units // 3) * unit
    packed = jnp.concatenate([grad.astype(BFLOAT) for grad in grads[:4]], axis=0)
    packed = jnp.pad(packed, ((0, units * unit - 4 * width), (0, 0)))
    pieces, orders = [packed[:cut], small], [("dp", "context", "experts")] * 2
    if cut < units * unit:
        pieces.append(packed[cut:])
        orders.append(("dp", "experts", "context"))
    pieces = reduce_all(pieces, orders, 4)
    packed = jnp.concatenate([pieces[0], *pieces[2:]], axis=0)
    summed = [packed[at * width : (at + 1) * width].astype(SINGLE) for at in range(4)]
    flat, at = pieces[1].reshape(-1), 0
    for grad in grads[4:]:
        summed.append(flat[at : at + grad.size].reshape(grad.shape))
        at += grad.size
    return (
        output.astype(BFLOAT)[None],
        grad_tokens[None],
        summed[0],
        summed[1],
        summed[2],
        summed[3],
        summed[4],
        summed[5],
        summed[6],
        summed[7],
        grad_w_in[0].astype(SINGLE),
        grad_w_out[0].astype(SINGLE),
    )


def solution(mesh):
    in_specs = (
        P(("experts", "dp"), "context", None),
        P(("experts", "dp"), "context", None),
        P(),
        P(),
        P(),
        P(),
        P(),
        P(),
        P(),
        P(),
        P("experts", None, None),
        P("experts", None, None),
        P(("experts", "dp"), "context"),
        P(("experts", "dp"), "context"),
        P(),
    )
    out_specs = (
        P(("experts", "dp"), "context", None),
        P(("experts", "dp"), "context", None),
        P(),
        P(),
        P(),
        P(),
        P(),
        P(),
        P(),
        P(),
        P("experts", None, ("context", "dp")),
        P("experts", ("context", "dp"), None),
    )
    return jax.shard_map(
        on_device, mesh=mesh, in_specs=in_specs, out_specs=out_specs, check_vma=False
    )
```

```python
import functools

import jax
import jax.numpy as jnp
from jax import lax
from jax.experimental import pallas as pl
from jax.experimental.pallas import tpu as pltpu
from jax.sharding import PartitionSpec as P

SINGLE = jnp.float32
BFLOAT = jnp.bfloat16
NT = (((1,), (1,)), ((), ()))
TN = (((0,), (0,)), ((), ()))


def rms_scale(value_rows, gain):
    return (
        value_rows
        * lax.rsqrt(jnp.mean(value_rows * value_rows, axis=-1, keepdims=True) + 1e-06)
        * gain
    )


def mm(left, right, dims=(((1,), (0,)), ((), ()))):
    return lax.dot_general(left, right, dims, preferred_element_type=SINGLE)


def lane_mask(shape, part, head_dim):
    return lax.broadcasted_iota(jnp.int32, shape, 1) // head_dim == part


def biased_scores(query, key, window_row):
    rows, cols = query.shape[0], key.shape[0]
    width = window_row.shape[1]
    spread = jnp.broadcast_to(window_row, (rows, width))
    shifted = pltpu.roll(spread, width - rows + 1, 1, stride=1, stride_axis=0)
    return mm(query, key, NT) + shifted[:, :cols]


def attend_kernel(head_dim, q_ref, k_ref, v_ref, win_ref, o_ref, lse_ref):
    query, key, value = q_ref[...], k_ref[...], v_ref[...]
    total = jnp.zeros(query.shape, SINGLE)
    for part in range(query.shape[1] // head_dim):
        mask = lane_mask(query.shape, part, head_dim)
        scores = biased_scores(jnp.where(mask, query, 0), key, win_ref[part])
        top = jnp.max(scores, axis=-1, keepdims=True)
        raised = jnp.exp(scores - top)
        summed = jnp.sum(raised, axis=-1, keepdims=True)
        lse_ref[part] = top + jnp.log(summed)
        probs = (raised * (1.0 / summed)).astype(BFLOAT)
        total = jnp.where(mask, mm(probs, value), total)
    o_ref[...] = total.astype(BFLOAT)


def attend_back_kernel(
    head_dim, q_ref, k_ref, v_ref, do_ref, lse_ref, win_ref, dq_ref, dkv_ref, diag_ref
):
    query, key, value, grad = q_ref[...], k_ref[...], v_ref[...], do_ref[...]
    rows, cols = query.shape[0], key.shape[0]
    blocks = cols // rows
    grad_q = jnp.zeros(query.shape, SINGLE)
    grad_k = jnp.zeros(key.shape, SINGLE)
    grad_v = jnp.zeros(key.shape, SINGLE)
    flip = (
        lax.broadcasted_iota(jnp.int32, (rows, rows), 0)
        + lax.broadcasted_iota(jnp.int32, (rows, rows), 1)
        == rows - 1
    ).astype(SINGLE).astype(BFLOAT)
    for part in range(query.shape[1] // head_dim):
        mask = lane_mask(query.shape, part, head_dim)
        mask_k = lane_mask(key.shape, part, head_dim)
        scores = biased_scores(jnp.where(mask, query, 0), key, win_ref[part])
        probs = jnp.exp(scores - lse_ref[part])
        grad_probs = mm(jnp.where(mask, grad, 0), value, NT)
        inner = jnp.sum(probs * grad_probs, axis=-1, keepdims=True)
        grad_scores = (probs * (grad_probs - inner)).astype(BFLOAT)
        grad_q = jnp.where(mask, mm(grad_scores, key), grad_q)
        grad_k = jnp.where(mask_k, mm(grad_scores, query, TN), grad_k)
        grad_v = jnp.where(mask_k, mm(probs.astype(BFLOAT), grad, TN), grad_v)
        turned = jnp.concatenate(
            [mm(flip, grad_scores), jnp.zeros((rows, rows), SINGLE)], axis=1
        )
        lined = pltpu.roll(turned, 0, 1, stride=1, stride_axis=0)
        diag_ref[part] = jnp.sum(lined, axis=0, keepdims=True)
    dq_ref[...] = grad_q.astype(BFLOAT)
    grad_k, grad_v = grad_k.astype(BFLOAT), grad_v.astype(BFLOAT)
    for block in range(blocks):
        dkv_ref[block, 0] = grad_k[block * rows : (block + 1) * rows]
        dkv_ref[block, 1] = grad_v[block * rows : (block + 1) * rows]


def attention_specs(rows, cols, lanes, parts, pairs, span):
    return dict(
        q=pl.BlockSpec((rows, lanes), lambda p: (0, p)),
        k=pl.BlockSpec((cols, lanes), lambda p: (0, p)),
        v=pl.BlockSpec((cols, lanes), lambda p: (0, p + pairs)),
        win=pl.BlockSpec((parts, 1, span), lambda p: (p, 0, 0)),
        lse=pl.BlockSpec((parts, rows, 1), lambda p: (p, 0, 0)),
    )


def attend(query, pair_all, window, head_dim):
    rows, width = query.shape
    cols, heads, span = pair_all.shape[0], window.shape[0], window.shape[2]
    lanes = max(128, head_dim)
    pairs, parts = width // lanes, lanes // head_dim
    spec = attention_specs(rows, cols, lanes, parts, pairs, span)
    return pl.pallas_call(
        functools.partial(attend_kernel, head_dim),
        grid=(pairs,),
        in_specs=[spec["q"], spec["k"], spec["v"], spec["win"]],
        out_specs=[spec["q"], spec["lse"]],
        out_shape=[
            jax.ShapeDtypeStruct((rows, width), BFLOAT),
            jax.ShapeDtypeStruct((heads, rows, 1), SINGLE),
        ],
        compiler_params=pltpu.CompilerParams(vmem_limit_bytes=40 * 2**20),
        cost_estimate=pl.CostEstimate(
            flops=4 * rows * cols * width,
            bytes_accessed=4 * cols * width + 4 * rows * width,
            transcendentals=heads * rows * cols,
        ),
    )(query, pair_all, pair_all, window)


def attend_back(query, pair_all, grad, lse, window, head_dim):
    rows, width = query.shape
    cols, heads, span = pair_all.shape[0], window.shape[0], window.shape[2]
    lanes = max(128, head_dim)
    pairs, parts = width // lanes, lanes // head_dim
    spec = attention_specs(rows, cols, lanes, parts, pairs, span)
    blocks = cols // rows
    return pl.pallas_call(
        functools.partial(attend_back_kernel, head_dim),
        grid=(pairs,),
        in_specs=[spec["q"], spec["k"], spec["v"], spec["q"], spec["lse"], spec["win"]],
        out_specs=[
            spec["q"],
            pl.BlockSpec((blocks, 2, rows, lanes), lambda p: (0, 0, 0, p)),
            spec["win"],
        ],
        out_shape=[
            jax.ShapeDtypeStruct((rows, width), BFLOAT),
            jax.ShapeDtypeStruct((blocks, 2, rows, width), BFLOAT),
            jax.ShapeDtypeStruct((heads, 1, span), SINGLE),
        ],
        compiler_params=pltpu.CompilerParams(vmem_limit_bytes=48 * 2**20),
        cost_estimate=pl.CostEstimate(
            flops=12 * rows * cols * width,
            bytes_accessed=8 * cols * width + 8 * rows * width,
            transcendentals=heads * rows * cols,
        ),
    )(query, pair_all, pair_all, grad, lse, window)


MESH = pl.DeviceIdType.MESH
ANY = pl.BlockSpec(memory_space=pl.ANY)
VMEM = pl.BlockSpec(memory_space=pltpu.VMEM)


def greet(peers):
    barrier = pltpu.get_barrier_semaphore()
    for peer in peers:
        pl.semaphore_signal(barrier, inc=1, device_id=peer, device_id_type=MESH)
    pl.semaphore_wait(barrier, len(peers))


def remote(src, dst, send_sem, recv_sem, peer):
    copy = pltpu.make_async_remote_copy(
        src_ref=src,
        dst_ref=dst,
        send_sem=send_sem,
        recv_sem=recv_sem,
        device_id=peer,
        device_id_type=MESH,
    )
    copy.start()
    return copy


def add_tiles(rows, own, others, store):
    tile = 64 if rows % 64 == 0 else rows

    def add(step, carry):
        at = pl.ds(pl.multiple_of(step * tile, tile), tile)
        total = own(step * tile, tile)
        for other in others:
            total = total + other[at].astype(SINGLE)
        store(step * tile, tile, total)
        return carry

    lax.fori_loop(0, rows // tile, add, 0)


def swap_kernel(axis, count, gather, x_ref, o_ref, send_sem, recv_sem, own_sem):
    me = lax.axis_index(axis)
    peers = [lax.rem(me + step, count) for step in range(1, count)]
    greet([{axis: peer} for peer in peers])
    copies = [
        remote(
            x_ref if gather else x_ref.at[peer],
            o_ref.at[me],
            send_sem.at[at],
            recv_sem.at[at],
            {axis: peer},
        )
        for at, peer in enumerate(peers)
    ]
    own = pltpu.make_async_copy(x_ref if gather else x_ref.at[me], o_ref.at[me], own_sem)
    own.start()
    own.wait()
    for copy in copies:
        copy.wait()


def swap(x, axis, collective_id, gather=False):
    count = lax.axis_size(axis)
    shape = (count, *x.shape) if gather else x.shape
    return pl.pallas_call(
        functools.partial(swap_kernel, axis, count, gather),
        in_specs=[ANY],
        out_specs=ANY,
        out_shape=jax.ShapeDtypeStruct(shape, x.dtype),
        scratch_shapes=[
            pltpu.SemaphoreType.DMA((count - 1,)),
            pltpu.SemaphoreType.DMA((count - 1,)),
            pltpu.SemaphoreType.DMA,
        ],
        compiler_params=pltpu.CompilerParams(collective_id=collective_id, has_side_effects=True),
    )(x)


def reduce_kernel(orders, sizes, backs, *refs):
    count = len(orders)
    x_refs, o_refs, scratch = refs[:count], refs[count : 2 * count], refs[2 * count :]
    send_sem, recv_sem = scratch[-2:]
    me = {axis: lax.axis_index(axis) for axis in sizes}
    peers = {
        axis: [lax.rem(me[axis] + step, size) for step in range(1, size)]
        for axis, size in sizes.items()
    }
    greet([{axis: peer} for axis in sizes for peer in peers[axis]])
    held, part, chunks, places, spot = [], [], [], [], 0
    for order in orders:
        held.append(scratch[spot : spot + len(order)])
        part.append(scratch[spot + len(order) : spot + 2 * len(order)])
        spot += 2 * len(order)
    for at, order in enumerate(orders):
        rows, place, own_chunks, own_places = x_refs[at].shape[0], 0, [], []
        for axis in order:
            rows = rows // sizes[axis]
            place = place + me[axis] * rows
            own_chunks.append(rows)
            own_places.append(place)
        chunks.append(own_chunks)
        places.append(own_places)

    def begin(at, phase):
        depth = len(orders[at])
        level = phase if phase < depth else 2 * depth - 1 - phase
        axis, chunk = orders[at][level], chunks[at][level]
        copies = []
        for slot, peer in enumerate(peers[axis]):
            if phase < depth:
                source = x_refs[at] if level == 0 else part[at][level - 1]
                src = source.at[pl.ds(pl.multiple_of(peer * chunk, chunk), chunk)]
                dst = held[at][level].at[slot]
            else:
                where = pl.ds(pl.multiple_of(places[at][level], chunk), chunk)
                src = dst = o_refs[at].at[where]
            sems = send_sem.at[at, phase, slot], recv_sem.at[at, phase, slot]
            copies.append(remote(src, dst, *sems, {axis: peer}))
        return copies

    def finish(at, phase, copies):
        for copy in copies:
            copy.wait()
        depth = len(orders[at])
        if phase >= depth:
            return
        axis, chunk = orders[at][phase], chunks[at][phase]
        source = x_refs[at] if phase == 0 else part[at][phase - 1]
        last = phase == depth - 1
        target = o_refs[at] if last else part[at][phase]
        base = pl.multiple_of(places[at][phase], chunk) if last and backs[at] else 0
        start = me[axis] * chunk

        def load(row, tile):
            return source[pl.ds(pl.multiple_of(start + row, tile), tile)].astype(SINGLE)

        def store(row, tile, total):
            target[pl.ds(pl.multiple_of(base + row, tile), tile)] = total.astype(target.dtype)

        add_tiles(chunk, load, [held[at][phase].at[slot] for slot in range(len(peers[axis]))], store)

    flying = [None] * count
    phases = [len(order) * (2 if back else 1) for order, back in zip(orders, backs)]
    for phase in range(max(phases) + 1):
        for at in range(count):
            if 0 < phase <= phases[at]:
                finish(at, phase - 1, flying[at])
            if phase < phases[at]:
                flying[at] = begin(at, phase)


def reduce_all(pieces, orders, backs, collective_id):
    sizes = {axis: lax.axis_size(axis) for order in orders for axis in order}
    scratch, shapes = [], []
    for piece, order, back in zip(pieces, orders, backs):
        rows, width = piece.shape
        held, part = [], []
        for axis in order:
            rows = rows // sizes[axis]
            held.append(pltpu.VMEM((sizes[axis] - 1, rows, width), piece.dtype))
            part.append(pltpu.VMEM((rows, width), piece.dtype))
        scratch += held + part
        shapes.append((piece.shape[0] if back else rows, width))
    sems = (len(pieces), 2 * len(sizes), max(sizes.values()) - 1)
    return pl.pallas_call(
        functools.partial(reduce_kernel, orders, sizes, backs),
        in_specs=[VMEM] * len(pieces),
        out_specs=[VMEM] * len(pieces),
        out_shape=[
            jax.ShapeDtypeStruct(shape, piece.dtype) for shape, piece in zip(shapes, pieces)
        ],
        scratch_shapes=scratch + [pltpu.SemaphoreType.DMA(sems), pltpu.SemaphoreType.DMA(sems)],
        compiler_params=pltpu.CompilerParams(
            collective_id=collective_id, has_side_effects=True, vmem_limit_bytes=48 * 2**20
        ),
    )(*pieces)


def pack(grads, unit):
    packed = jnp.concatenate([grad.astype(BFLOAT) for grad in grads], axis=0)
    return jnp.pad(packed, ((0, -packed.shape[0] % unit), (0, 0)))


def gelu_both(pre):
    root = 0.7978845608028654
    square = pre * pre
    bend = jnp.tanh(root * (pre + 0.044715 * square * pre))
    half = 0.5 * (1.0 + bend)
    slope = half + 0.5 * pre * (1.0 - bend * bend) * root * (1.0 + 0.134145 * square)
    return pre * half, slope


def expert_kernel(
    axis, count, shares, x_ref, win_ref, wout_ref, back_ref, gin_ref, gout_ref,
    arrived, leaving, w_in, w_out, act, grad_pre, total, grad_total, whole_in, whole_out,
    send_sem, recv_sem, own_sem, load_sem, store_sem,
):
    experts, _, capacity, both = arrived.shape
    width, hidden, rows = both // 2, w_in.shape[2], count * capacity
    share = hidden // shares
    me = lax.axis_index(axis)
    peers = [lax.rem(me + step, count) for step in range(1, count)]
    greet([{axis: peer} for peer in peers])
    loads, coming = [], []
    for e in range(experts):
        here = [
            remote(
                x_ref.at[peer, e], arrived.at[e, me],
                send_sem.at[0, e, at], recv_sem.at[0, e, at], {axis: peer},
            )
            for at, peer in enumerate(peers)
        ]
        own = pltpu.make_async_copy(x_ref.at[me, e], arrived.at[e, me], own_sem.at[0, e])
        own.start()
        coming.append(here + [own])
    for e in range(experts):
        pair = [
            pltpu.make_async_copy(win_ref.at[e], w_in.at[e], load_sem.at[0, e]),
            pltpu.make_async_copy(wout_ref.at[e], w_out.at[e], load_sem.at[1, e]),
        ]
        for copy in pair:
            copy.start()
        loads.append(pair)
    tile = 512 if hidden % 512 == 0 else hidden
    leave, stores = [], []
    for e in range(experts):
        for copy in coming[e] + loads[e]:
            copy.wait()
        landed = arrived[e].astype(SINGLE).reshape(rows, both).astype(BFLOAT)
        came, grad = landed[:, :width], landed[:, width:]
        total[...] = jnp.zeros_like(total)
        grad_total[...] = jnp.zeros_like(grad_total)

        def step(at, carry):
            cut = pl.ds(pl.multiple_of(at * tile, tile), tile)
            into, out = w_in[e, :, cut], w_out[e, cut, :]
            value, slope = gelu_both(mm(came, into))
            value = value.astype(BFLOAT)
            act[:, cut] = value
            total[...] += mm(value, out)
            turned = (mm(grad, out, NT) * slope).astype(BFLOAT)
            grad_pre[:, cut] = turned
            grad_total[...] += mm(turned, into, NT)
            return carry

        lax.fori_loop(0, hidden // tile, step, 0)
        leaving[e, :, :, :width] = total[...].reshape(count, capacity, width).astype(BFLOAT)
        leaving[e, :, :, width:] = grad_total[...].reshape(count, capacity, width).astype(BFLOAT)
        leave += [
            remote(
                leaving.at[e, peer], back_ref.at[me, e],
                send_sem.at[1, e, at], recv_sem.at[1, e, at], {axis: peer},
            )
            for at, peer in enumerate(peers)
        ]
        own = pltpu.make_async_copy(leaving.at[e, me], back_ref.at[me, e], own_sem.at[1, e])
        own.start()
        leave.append(own)

        def weigh(at, carry):
            cut = pl.ds(pl.multiple_of(at * share, share), share)
            whole_in[e, at] = mm(came, grad_pre[:, cut], TN).astype(BFLOAT)
            whole_out[e, at] = mm(act[:, cut], grad, TN).astype(BFLOAT)
            return carry

        lax.fori_loop(0, shares, weigh, 0)
        pair = [
            pltpu.make_async_copy(whole_in.at[e], gin_ref.at[:, e], store_sem.at[0, e]),
            pltpu.make_async_copy(whole_out.at[e], gout_ref.at[:, e], store_sem.at[1, e]),
        ]
        for copy in pair:
            copy.start()
        stores += pair
    for copy in leave + stores:
        copy.wait()


def expert_layer(x, w_in, w_out, axis, shares, collective_id):
    count, experts, capacity, both = x.shape
    width, hidden = w_in.shape[1:]
    rows, share = count * capacity, hidden // shares
    landed = pltpu.VMEM((experts, count, capacity, both), BFLOAT)
    flat = pltpu.VMEM((rows, hidden), BFLOAT)
    sums = pltpu.VMEM((rows, width), SINGLE)
    return pl.pallas_call(
        functools.partial(expert_kernel, axis, count, shares),
        in_specs=[ANY] * 3,
        out_specs=[ANY] * 3,
        out_shape=[
            jax.ShapeDtypeStruct(x.shape, BFLOAT),
            jax.ShapeDtypeStruct((shares, experts, width, share), BFLOAT),
            jax.ShapeDtypeStruct((shares, experts, share, width), BFLOAT),
        ],
        scratch_shapes=[
            landed,
            landed,
            pltpu.VMEM(w_in.shape, BFLOAT),
            pltpu.VMEM(w_out.shape, BFLOAT),
            flat,
            flat,
            sums,
            sums,
            pltpu.VMEM((experts, shares, width, share), BFLOAT),
            pltpu.VMEM((experts, shares, share, width), BFLOAT),
            pltpu.SemaphoreType.DMA((2, experts, count - 1)),
            pltpu.SemaphoreType.DMA((2, experts, count - 1)),
            pltpu.SemaphoreType.DMA((2, experts)),
            pltpu.SemaphoreType.DMA((2, experts)),
            pltpu.SemaphoreType.DMA((2, experts)),
        ],
        compiler_params=pltpu.CompilerParams(
            collective_id=collective_id, has_side_effects=True, vmem_limit_bytes=58 * 2**20
        ),
        cost_estimate=pl.CostEstimate(
            flops=12 * experts * rows * width * hidden,
            bytes_accessed=8 * experts * width * hidden,
            transcendentals=experts * rows * hidden,
        ),
    )(x, w_in, w_out)


def on_device(
    tokens,
    cotangent,
    w_query,
    w_key,
    w_value,
    w_output,
    gain_attn,
    gain_ffn,
    bias_table,
    w_router,
    w_in,
    w_out,
    routes,
    slots,
    buckets,
):
    tok_count = tokens.shape[1]
    width = tokens.shape[2]
    heads = bias_table.shape[1]
    bucket_count = bias_table.shape[0]
    head_dim = width // heads
    n_context = lax.axis_size("context")
    seq_len = tok_count * n_context
    n_owner = lax.axis_size("experts")
    shares = n_context * lax.axis_size("dp")
    expert_dev = w_in.shape[0]
    capacity = 2 * tok_count // (expert_dev * n_owner)
    highest = lax.Precision.HIGHEST
    resid = tokens[0].astype(SINGLE)
    first_norm_output = rms_scale(resid, gain_attn).astype(BFLOAT)
    pair_bf = jnp.concatenate(
        [mm(first_norm_output, w_key).astype(BFLOAT), mm(first_norm_output, w_value).astype(BFLOAT)],
        axis=1,
    )
    pair_all = swap(pair_bf, "context", 0, gather=True).reshape(seq_len, 2 * width)
    query_bf = mm(first_norm_output, w_query).astype(BFLOAT)
    span = seq_len + tok_count
    first = seq_len - (lax.axis_index("context") + 1) * tok_count
    bucket_window = lax.dynamic_slice(jnp.pad(buckets, (0, 1)), (first,), (span,))
    window_hot = (
        bucket_window[:, None] == jnp.arange(bucket_count, dtype=jnp.int32)[None, :]
    ).astype(SINGLE)
    window = jnp.einsum("ob,bh->ho", window_hot, bias_table, precision=highest)[:, None, :]
    attention_result, log_total = attend(query_bf, pair_all, window, head_dim)
    residual_middle = resid + mm(attention_result, w_output)
    norm_two = rms_scale(residual_middle, gain_ffn)
    logits = jnp.dot(norm_two, w_router, precision=highest)
    route_probs = jax.nn.softmax(logits, axis=-1)
    route_row = routes[0]
    slot_row = slots[0]
    route_hot = (
        route_row[:, None] == jnp.arange(logits.shape[1], dtype=jnp.int32)[None, :]
    ).astype(SINGLE)
    gate = jnp.sum(route_probs * route_hot, axis=-1)
    grad_out = cotangent[0].astype(SINGLE)
    grad_routed = (grad_out * gate[:, None]).astype(BFLOAT)
    slot_count = expert_dev * n_owner * capacity
    layout = (
        route_row // expert_dev * (expert_dev * capacity)
        + route_row % expert_dev * capacity
        + slot_row
    )
    place = jnp.where(slot_row < capacity, layout, -1)
    slot_hot = (place[:, None] == jnp.arange(slot_count, dtype=jnp.int32)[None, :]).astype(BFLOAT)
    send = mm(
        slot_hot, jnp.concatenate([norm_two.astype(BFLOAT), grad_routed], axis=1), TN
    ).astype(BFLOAT)
    returned, whole_in, whole_out = expert_layer(
        send.reshape(n_owner, expert_dev, capacity, 2 * width), w_in, w_out, "experts", shares, 1
    )
    returned = returned.reshape(slot_count, 2 * width)
    grad_w_in = lax.psum_scatter(whole_in, ("context", "dp"), scatter_dimension=0, tiled=True)
    grad_w_out = lax.psum_scatter(whole_out, ("context", "dp"), scatter_dimension=0, tiled=True)
    fetched = mm(slot_hot, returned)
    routed = fetched[:, :width]
    output = residual_middle + gate[:, None] * routed
    grad_gate = jnp.sum(grad_out * routed, axis=-1)
    grad_logits = grad_gate[:, None] * route_probs * (route_hot - gate[:, None])
    grad_router = jnp.einsum("td,te->de", norm_two, grad_logits, precision=highest)
    grad_norm_two = fetched[:, width:] + jnp.einsum(
        "te,de->td", grad_logits, w_router, precision=highest
    )
    grad_mid, grad_gain_ffn = jax.vjp(rms_scale, residual_middle, gain_ffn)[1](grad_norm_two)
    grad_mid = grad_mid + grad_out
    grad_attn = grad_mid.astype(BFLOAT)
    grad_output = mm(attention_result, grad_attn, TN)
    grad_attended = mm(grad_attn, w_output, NT).astype(BFLOAT)
    grad_q, grad_pair, diagonal = attend_back(
        query_bf, pair_all, grad_attended, log_total, window, head_dim
    )
    grad_query = mm(first_norm_output, grad_q, TN)
    unit = 16 * n_owner * shares
    grad_pair, early = reduce_all(
        [grad_pair.reshape(2 * seq_len, width), pack([grad_query, grad_output], unit)],
        [("context",), ("dp", "experts", "context")],
        [False, True],
        2,
    )
    grad_k, grad_v = grad_pair[:tok_count], grad_pair[tok_count:]
    grad_table = jnp.einsum("ho,ob->bh", diagonal[:, 0, :], window_hot, precision=highest)
    grad_key = mm(first_norm_output, grad_k, TN)
    grad_value = mm(first_norm_output, grad_v, TN)
    grad_norm_one = mm(grad_q, w_query, NT) + mm(grad_k, w_key, NT) + mm(grad_v, w_value, NT)
    grad_resid, grad_gain_attn = jax.vjp(rms_scale, resid, gain_attn)[1](grad_norm_one)
    grad_tokens = grad_resid + grad_mid
    grads = (grad_gain_attn, grad_gain_ffn, grad_table, grad_router)
    small = jnp.concatenate([grad.reshape(-1) for grad in grads])
    small_rows = -(-small.shape[0] // (64 * unit)) * (unit // 2)
    small = jnp.pad(small, (0, small_rows * 128 - small.shape[0])).reshape(small_rows, 128)
    late = pack([grad_key, grad_value], unit)
    cut = -(-2 * late.shape[0] // (3 * unit)) * unit
    pieces, orders = [late[:cut], small], [("dp", "context", "experts")] * 2
    if cut < late.shape[0]:
        pieces.append(late[cut:])
        orders.append(("dp", "experts", "context"))
    pieces = reduce_all(pieces, orders, [True] * len(pieces), 3)
    late = jnp.concatenate([pieces[0], *pieces[2:]], axis=0)
    summed = []
    for packed in (early, late):
        summed += [packed[:width].astype(SINGLE), packed[width : 2 * width].astype(SINGLE)]
    summed = [summed[0], summed[2], summed[3], summed[1]]
    flat, at = pieces[1].reshape(-1), 0
    for grad in grads:
        summed.append(flat[at : at + grad.size].reshape(grad.shape))
        at += grad.size
    return (
        output.astype(BFLOAT)[None],
        grad_tokens[None],
        summed[0],
        summed[1],
        summed[2],
        summed[3],
        summed[4],
        summed[5],
        summed[6],
        summed[7],
        grad_w_in[0].astype(SINGLE),
        grad_w_out[0].astype(SINGLE),
    )


def solution(mesh):
    in_specs = (
        P(("experts", "dp"), "context", None),
        P(("experts", "dp"), "context", None),
        P(),
        P(),
        P(),
        P(),
        P(),
        P(),
        P(),
        P(),
        P("experts", None, None),
        P("experts", None, None),
        P(("experts", "dp"), "context"),
        P(("experts", "dp"), "context"),
        P(),
    )
    out_specs = (
        P(("experts", "dp"), "context", None),
        P(("experts", "dp"), "context", None),
        P(),
        P(),
        P(),
        P(),
        P(),
        P(),
        P(),
        P(),
        P("experts", None, ("context", "dp")),
        P("experts", ("context", "dp"), None),
    )
    return jax.shard_map(
        on_device, mesh=mesh, in_specs=in_specs, out_specs=out_specs, check_vma=False
    )
```

```python
import functools

import jax
import jax.numpy as jnp
from jax import lax
from jax.experimental import pallas as pl
from jax.experimental.pallas import tpu as pltpu
from jax.sharding import PartitionSpec as P

SINGLE = jnp.float32
BFLOAT = jnp.bfloat16
NT = (((1,), (1,)), ((), ()))
TN = (((0,), (0,)), ((), ()))


def rms_scale(value_rows, gain):
    return (
        value_rows
        * lax.rsqrt(jnp.mean(value_rows * value_rows, axis=-1, keepdims=True) + 1e-06)
        * gain
    )


def mm(left, right, dims=(((1,), (0,)), ((), ()))):
    return lax.dot_general(left, right, dims, preferred_element_type=SINGLE)


def lane_mask(shape, part, head_dim):
    return lax.broadcasted_iota(jnp.int32, shape, 1) // head_dim == part


def biased_scores(query, key, window_row):
    rows, cols = query.shape[0], key.shape[0]
    width = window_row.shape[1]
    spread = jnp.broadcast_to(window_row, (rows, width))
    shifted = pltpu.roll(spread, width - rows + 1, 1, stride=1, stride_axis=0)
    return mm(query, key, NT) + shifted[:, :cols]


def attend_kernel(head_dim, q_ref, k_ref, v_ref, win_ref, o_ref, lse_ref):
    query, key, value = q_ref[...], k_ref[...], v_ref[...]
    total = jnp.zeros(query.shape, SINGLE)
    for part in range(query.shape[1] // head_dim):
        mask = lane_mask(query.shape, part, head_dim)
        scores = biased_scores(jnp.where(mask, query, 0), key, win_ref[part])
        top = jnp.max(scores, axis=-1, keepdims=True)
        raised = jnp.exp(scores - top)
        summed = jnp.sum(raised, axis=-1, keepdims=True)
        lse_ref[part] = top + jnp.log(summed)
        probs = (raised * (1.0 / summed)).astype(BFLOAT)
        total = jnp.where(mask, mm(probs, value), total)
    o_ref[...] = total.astype(BFLOAT)


def attend_back_kernel(
    head_dim, q_ref, k_ref, v_ref, do_ref, lse_ref, win_ref, dq_ref, dkv_ref, diag_ref
):
    query, key, value, grad = q_ref[...], k_ref[...], v_ref[...], do_ref[...]
    rows, cols = query.shape[0], key.shape[0]
    blocks = cols // rows
    grad_q = jnp.zeros(query.shape, SINGLE)
    grad_k = jnp.zeros(key.shape, SINGLE)
    grad_v = jnp.zeros(key.shape, SINGLE)
    flip = (
        lax.broadcasted_iota(jnp.int32, (rows, rows), 0)
        + lax.broadcasted_iota(jnp.int32, (rows, rows), 1)
        == rows - 1
    ).astype(SINGLE).astype(BFLOAT)
    for part in range(query.shape[1] // head_dim):
        mask = lane_mask(query.shape, part, head_dim)
        mask_k = lane_mask(key.shape, part, head_dim)
        scores = biased_scores(jnp.where(mask, query, 0), key, win_ref[part])
        probs = jnp.exp(scores - lse_ref[part])
        grad_probs = mm(jnp.where(mask, grad, 0), value, NT)
        inner = jnp.sum(probs * grad_probs, axis=-1, keepdims=True)
        grad_scores = (probs * (grad_probs - inner)).astype(BFLOAT)
        grad_q = jnp.where(mask, mm(grad_scores, key), grad_q)
        grad_k = jnp.where(mask_k, mm(grad_scores, query, TN), grad_k)
        grad_v = jnp.where(mask_k, mm(probs.astype(BFLOAT), grad, TN), grad_v)
        turned = jnp.concatenate(
            [mm(flip, grad_scores), jnp.zeros((rows, rows), SINGLE)], axis=1
        )
        lined = pltpu.roll(turned, 0, 1, stride=1, stride_axis=0)
        diag_ref[part] = jnp.sum(lined, axis=0, keepdims=True)
    dq_ref[...] = grad_q.astype(BFLOAT)
    grad_k, grad_v = grad_k.astype(BFLOAT), grad_v.astype(BFLOAT)
    for block in range(blocks):
        dkv_ref[block, 0] = grad_k[block * rows : (block + 1) * rows]
        dkv_ref[block, 1] = grad_v[block * rows : (block + 1) * rows]


def attention_specs(rows, cols, lanes, parts, pairs, span):
    return dict(
        q=pl.BlockSpec((rows, lanes), lambda p: (0, p)),
        k=pl.BlockSpec((cols, lanes), lambda p: (0, p)),
        v=pl.BlockSpec((cols, lanes), lambda p: (0, p + pairs)),
        win=pl.BlockSpec((parts, 1, span), lambda p: (p, 0, 0)),
        lse=pl.BlockSpec((parts, rows, 1), lambda p: (p, 0, 0)),
    )


def attend(query, pair_all, window, head_dim):
    rows, width = query.shape
    cols, heads, span = pair_all.shape[0], window.shape[0], window.shape[2]
    lanes = max(128, head_dim)
    pairs, parts = width // lanes, lanes // head_dim
    spec = attention_specs(rows, cols, lanes, parts, pairs, span)
    return pl.pallas_call(
        functools.partial(attend_kernel, head_dim),
        grid=(pairs,),
        in_specs=[spec["q"], spec["k"], spec["v"], spec["win"]],
        out_specs=[spec["q"], spec["lse"]],
        out_shape=[
            jax.ShapeDtypeStruct((rows, width), BFLOAT),
            jax.ShapeDtypeStruct((heads, rows, 1), SINGLE),
        ],
        compiler_params=pltpu.CompilerParams(vmem_limit_bytes=40 * 2**20),
        cost_estimate=pl.CostEstimate(
            flops=4 * rows * cols * width,
            bytes_accessed=4 * cols * width + 4 * rows * width,
            transcendentals=heads * rows * cols,
        ),
    )(query, pair_all, pair_all, window)


def attend_back(query, pair_all, grad, lse, window, head_dim):
    rows, width = query.shape
    cols, heads, span = pair_all.shape[0], window.shape[0], window.shape[2]
    lanes = max(128, head_dim)
    pairs, parts = width // lanes, lanes // head_dim
    spec = attention_specs(rows, cols, lanes, parts, pairs, span)
    blocks = cols // rows
    return pl.pallas_call(
        functools.partial(attend_back_kernel, head_dim),
        grid=(pairs,),
        in_specs=[spec["q"], spec["k"], spec["v"], spec["q"], spec["lse"], spec["win"]],
        out_specs=[
            spec["q"],
            pl.BlockSpec((blocks, 2, rows, lanes), lambda p: (0, 0, 0, p)),
            spec["win"],
        ],
        out_shape=[
            jax.ShapeDtypeStruct((rows, width), BFLOAT),
            jax.ShapeDtypeStruct((blocks, 2, rows, width), BFLOAT),
            jax.ShapeDtypeStruct((heads, 1, span), SINGLE),
        ],
        compiler_params=pltpu.CompilerParams(vmem_limit_bytes=48 * 2**20),
        cost_estimate=pl.CostEstimate(
            flops=12 * rows * cols * width,
            bytes_accessed=8 * cols * width + 8 * rows * width,
            transcendentals=heads * rows * cols,
        ),
    )(query, pair_all, pair_all, grad, lse, window)


MESH = pl.DeviceIdType.MESH
ANY = pl.BlockSpec(memory_space=pl.ANY)
VMEM = pl.BlockSpec(memory_space=pltpu.VMEM)


def greet(peers):
    barrier = pltpu.get_barrier_semaphore()
    for peer in peers:
        pl.semaphore_signal(barrier, inc=1, device_id=peer, device_id_type=MESH)
    pl.semaphore_wait(barrier, len(peers))


def remote(src, dst, send_sem, recv_sem, peer):
    copy = pltpu.make_async_remote_copy(
        src_ref=src,
        dst_ref=dst,
        send_sem=send_sem,
        recv_sem=recv_sem,
        device_id=peer,
        device_id_type=MESH,
    )
    copy.start()
    return copy


def add_tiles(rows, own, others, store):
    tile = 64 if rows % 64 == 0 else rows

    def add(step, carry):
        at = pl.ds(pl.multiple_of(step * tile, tile), tile)
        total = own(step * tile, tile)
        for other in others:
            total = total + other[at].astype(SINGLE)
        store(step * tile, tile, total)
        return carry

    lax.fori_loop(0, rows // tile, add, 0)


def swap_kernel(axis, count, gather, x_ref, o_ref, send_sem, recv_sem, own_sem):
    me = lax.axis_index(axis)
    peers = [lax.rem(me + step, count) for step in range(1, count)]
    greet([{axis: peer} for peer in peers])
    copies = [
        remote(
            x_ref if gather else x_ref.at[peer],
            o_ref.at[me],
            send_sem.at[at],
            recv_sem.at[at],
            {axis: peer},
        )
        for at, peer in enumerate(peers)
    ]
    own = pltpu.make_async_copy(x_ref if gather else x_ref.at[me], o_ref.at[me], own_sem)
    own.start()
    own.wait()
    for copy in copies:
        copy.wait()


def swap(x, axis, collective_id, gather=False):
    count = lax.axis_size(axis)
    shape = (count, *x.shape) if gather else x.shape
    return pl.pallas_call(
        functools.partial(swap_kernel, axis, count, gather),
        in_specs=[ANY],
        out_specs=ANY,
        out_shape=jax.ShapeDtypeStruct(shape, x.dtype),
        scratch_shapes=[
            pltpu.SemaphoreType.DMA((count - 1,)),
            pltpu.SemaphoreType.DMA((count - 1,)),
            pltpu.SemaphoreType.DMA,
        ],
        compiler_params=pltpu.CompilerParams(collective_id=collective_id, has_side_effects=True),
    )(x)


def reduce_kernel(orders, sizes, backs, *refs):
    count = len(orders)
    x_refs, o_refs, scratch = refs[:count], refs[count : 2 * count], refs[2 * count :]
    send_sem, recv_sem = scratch[-2:]
    me = {axis: lax.axis_index(axis) for axis in sizes}
    peers = {
        axis: [lax.rem(me[axis] + step, size) for step in range(1, size)]
        for axis, size in sizes.items()
    }
    greet([{axis: peer} for axis in sizes for peer in peers[axis]])
    held, part, chunks, places, spot = [], [], [], [], 0
    for order in orders:
        held.append(scratch[spot : spot + len(order)])
        part.append(scratch[spot + len(order) : spot + 2 * len(order)])
        spot += 2 * len(order)
    for at, order in enumerate(orders):
        rows, place, own_chunks, own_places = x_refs[at].shape[0], 0, [], []
        for axis in order:
            rows = rows // sizes[axis]
            place = place + me[axis] * rows
            own_chunks.append(rows)
            own_places.append(place)
        chunks.append(own_chunks)
        places.append(own_places)

    def begin(at, phase):
        depth = len(orders[at])
        level = phase if phase < depth else 2 * depth - 1 - phase
        axis, chunk = orders[at][level], chunks[at][level]
        copies = []
        for slot, peer in enumerate(peers[axis]):
            if phase < depth:
                source = x_refs[at] if level == 0 else part[at][level - 1]
                src = source.at[pl.ds(pl.multiple_of(peer * chunk, chunk), chunk)]
                dst = held[at][level].at[slot]
            else:
                where = pl.ds(pl.multiple_of(places[at][level], chunk), chunk)
                src = dst = o_refs[at].at[where]
            sems = send_sem.at[at, phase, slot], recv_sem.at[at, phase, slot]
            copies.append(remote(src, dst, *sems, {axis: peer}))
        return copies

    def finish(at, phase, copies):
        for copy in copies:
            copy.wait()
        depth = len(orders[at])
        if phase >= depth:
            return
        axis, chunk = orders[at][phase], chunks[at][phase]
        source = x_refs[at] if phase == 0 else part[at][phase - 1]
        last = phase == depth - 1
        target = o_refs[at] if last else part[at][phase]
        base = pl.multiple_of(places[at][phase], chunk) if last and backs[at] else 0
        start = me[axis] * chunk

        def load(row, tile):
            return source[pl.ds(pl.multiple_of(start + row, tile), tile)].astype(SINGLE)

        def store(row, tile, total):
            target[pl.ds(pl.multiple_of(base + row, tile), tile)] = total.astype(target.dtype)

        add_tiles(chunk, load, [held[at][phase].at[slot] for slot in range(len(peers[axis]))], store)

    flying = [None] * count
    phases = [len(order) * (2 if back else 1) for order, back in zip(orders, backs)]
    for phase in range(max(phases) + 1):
        for at in range(count):
            if 0 < phase <= phases[at]:
                finish(at, phase - 1, flying[at])
            if phase < phases[at]:
                flying[at] = begin(at, phase)


def reduce_all(pieces, orders, backs, collective_id):
    sizes = {axis: lax.axis_size(axis) for order in orders for axis in order}
    scratch, shapes = [], []
    for piece, order, back in zip(pieces, orders, backs):
        rows, width = piece.shape
        held, part = [], []
        for axis in order:
            rows = rows // sizes[axis]
            held.append(pltpu.VMEM((sizes[axis] - 1, rows, width), piece.dtype))
            part.append(pltpu.VMEM((rows, width), piece.dtype))
        scratch += held + part
        shapes.append((piece.shape[0] if back else rows, width))
    sems = (len(pieces), 2 * len(sizes), max(sizes.values()) - 1)
    return pl.pallas_call(
        functools.partial(reduce_kernel, orders, sizes, backs),
        in_specs=[VMEM] * len(pieces),
        out_specs=[VMEM] * len(pieces),
        out_shape=[
            jax.ShapeDtypeStruct(shape, piece.dtype) for shape, piece in zip(shapes, pieces)
        ],
        scratch_shapes=scratch + [pltpu.SemaphoreType.DMA(sems), pltpu.SemaphoreType.DMA(sems)],
        compiler_params=pltpu.CompilerParams(
            collective_id=collective_id, has_side_effects=True, vmem_limit_bytes=48 * 2**20
        ),
    )(*pieces)


def pack(grads, unit):
    packed = jnp.concatenate([grad.astype(BFLOAT) for grad in grads], axis=0)
    return jnp.pad(packed, ((0, -packed.shape[0] % unit), (0, 0)))


def gelu_both(pre):
    root = 0.7978845608028654
    square = pre * pre
    bend = jnp.tanh(root * (pre + 0.044715 * square * pre))
    half = 0.5 * (1.0 + bend)
    slope = half + 0.5 * pre * (1.0 - bend * bend) * root * (1.0 + 0.134145 * square)
    return pre * half, slope


def expert_kernel(
    axis, count, shares, x_ref, win_ref, wout_ref, back_ref, own_ref, held_ref,
    arrived, leaving, w_in, w_out, act, grad_pre, total, grad_total, whole,
    send_sem, recv_sem, own_sem, load_sem, store_sem, half_sem,
):
    experts, _, capacity, both = arrived.shape
    width, hidden, rows = both // 2, w_in.shape[2], count * capacity
    share = hidden // shares
    me = lax.axis_index(axis)
    peers = [lax.rem(me + step, count) for step in range(1, count)]
    mine = lax.axis_index("dp")
    other = 1 - mine
    greet([{axis: peer} for peer in peers] + [{"dp": other}])
    loads, coming = [], []
    for e in range(experts):
        here = [
            remote(
                x_ref.at[peer, e], arrived.at[e, me],
                send_sem.at[0, e, at], recv_sem.at[0, e, at], {axis: peer},
            )
            for at, peer in enumerate(peers)
        ]
        own = pltpu.make_async_copy(x_ref.at[me, e], arrived.at[e, me], own_sem.at[0, e])
        own.start()
        coming.append(here + [own])
    for e in range(experts):
        pair = [
            pltpu.make_async_copy(win_ref.at[e], w_in.at[e], load_sem.at[0, e]),
            pltpu.make_async_copy(wout_ref.at[e], w_out.at[e], load_sem.at[1, e]),
        ]
        for copy in pair:
            copy.start()
        loads.append(pair)
    tile = 512 if hidden % 512 == 0 else hidden
    leave, stores = [], []
    for e in range(experts):
        for copy in coming[e] + loads[e]:
            copy.wait()
        landed = arrived[e].astype(SINGLE).reshape(rows, both).astype(BFLOAT)
        came, grad = landed[:, :width], landed[:, width:]
        total[...] = jnp.zeros_like(total)
        grad_total[...] = jnp.zeros_like(grad_total)

        def step(at, carry):
            cut = pl.ds(pl.multiple_of(at * tile, tile), tile)
            into, out = w_in[e, :, cut], w_out[e, cut, :]
            value, slope = gelu_both(mm(came, into))
            value = value.astype(BFLOAT)
            act[:, cut] = value
            total[...] += mm(value, out)
            turned = (mm(grad, out, NT) * slope).astype(BFLOAT)
            grad_pre[:, cut] = turned
            grad_total[...] += mm(turned, into, NT)
            return carry

        lax.fori_loop(0, hidden // tile, step, 0)
        leaving[e, :, :, :width] = total[...].reshape(count, capacity, width).astype(BFLOAT)
        leaving[e, :, :, width:] = grad_total[...].reshape(count, capacity, width).astype(BFLOAT)
        leave += [
            remote(
                leaving.at[e, peer], back_ref.at[me, e],
                send_sem.at[1, e, at], recv_sem.at[1, e, at], {axis: peer},
            )
            for at, peer in enumerate(peers)
        ]
        own = pltpu.make_async_copy(leaving.at[e, me], back_ref.at[me, e], own_sem.at[1, e])
        own.start()
        leave.append(own)

        def weigh(at, carry):
            cut = pl.ds(pl.multiple_of(at * share, share), share)
            half, place = lax.rem(at, 2), at // 2
            whole[e, half, place, 0] = mm(came, grad_pre[:, cut], TN).astype(BFLOAT)
            whole[e, half, place, 1] = mm(grad, act[:, cut], TN).astype(BFLOAT)
            return carry

        lax.fori_loop(0, shares, weigh, 0)
        stores.append(
            remote(
                whole.at[e, other], held_ref.at[e],
                half_sem.at[0, e], half_sem.at[1, e], {"dp": other},
            )
        )
        own = pltpu.make_async_copy(whole.at[e, mine], own_ref.at[e], store_sem.at[e])
        own.start()
        stores.append(own)
    for copy in leave + stores:
        copy.wait()


def expert_layer(x, w_in, w_out, axis, shares, collective_id):
    count, experts, capacity, both = x.shape
    width, hidden = w_in.shape[1:]
    rows, share = count * capacity, hidden // shares
    landed = pltpu.VMEM((experts, count, capacity, both), BFLOAT)
    flat = pltpu.VMEM((rows, hidden), BFLOAT)
    sums = pltpu.VMEM((rows, width), SINGLE)
    return pl.pallas_call(
        functools.partial(expert_kernel, axis, count, shares),
        in_specs=[ANY] * 3,
        out_specs=[ANY] * 3,
        out_shape=[
            jax.ShapeDtypeStruct(x.shape, BFLOAT),
            jax.ShapeDtypeStruct((experts, shares // 2, 2, width, share), BFLOAT),
            jax.ShapeDtypeStruct((experts, shares // 2, 2, width, share), BFLOAT),
        ],
        scratch_shapes=[
            landed,
            landed,
            pltpu.VMEM(w_in.shape, BFLOAT),
            pltpu.VMEM(w_out.shape, BFLOAT),
            flat,
            flat,
            sums,
            sums,
            pltpu.VMEM((experts, 2, shares // 2, 2, width, share), BFLOAT),
            pltpu.SemaphoreType.DMA((2, experts, count - 1)),
            pltpu.SemaphoreType.DMA((2, experts, count - 1)),
            pltpu.SemaphoreType.DMA((2, experts)),
            pltpu.SemaphoreType.DMA((2, experts)),
            pltpu.SemaphoreType.DMA((experts,)),
            pltpu.SemaphoreType.DMA((2, experts)),
        ],
        compiler_params=pltpu.CompilerParams(
            collective_id=collective_id, has_side_effects=True, vmem_limit_bytes=58 * 2**20
        ),
        cost_estimate=pl.CostEstimate(
            flops=12 * experts * rows * width * hidden,
            bytes_accessed=8 * experts * width * hidden,
            transcendentals=experts * rows * hidden,
        ),
    )(x, w_in, w_out)


def on_device(
    tokens,
    cotangent,
    w_query,
    w_key,
    w_value,
    w_output,
    gain_attn,
    gain_ffn,
    bias_table,
    w_router,
    w_in,
    w_out,
    routes,
    slots,
    buckets,
):
    tok_count = tokens.shape[1]
    width = tokens.shape[2]
    heads = bias_table.shape[1]
    bucket_count = bias_table.shape[0]
    head_dim = width // heads
    n_context = lax.axis_size("context")
    seq_len = tok_count * n_context
    n_owner = lax.axis_size("experts")
    shares = n_context * lax.axis_size("dp")
    expert_dev = w_in.shape[0]
    capacity = 2 * tok_count // (expert_dev * n_owner)
    highest = lax.Precision.HIGHEST
    resid = tokens[0].astype(SINGLE)
    first_norm_output = rms_scale(resid, gain_attn).astype(BFLOAT)
    pair_bf = jnp.concatenate(
        [mm(first_norm_output, w_key).astype(BFLOAT), mm(first_norm_output, w_value).astype(BFLOAT)],
        axis=1,
    )
    pair_all = swap(pair_bf, "context", 0, gather=True).reshape(seq_len, 2 * width)
    query_bf = mm(first_norm_output, w_query).astype(BFLOAT)
    span = seq_len + tok_count
    first = seq_len - (lax.axis_index("context") + 1) * tok_count
    bucket_window = lax.dynamic_slice(jnp.pad(buckets, (0, 1)), (first,), (span,))
    window_hot = (
        bucket_window[:, None] == jnp.arange(bucket_count, dtype=jnp.int32)[None, :]
    ).astype(SINGLE)
    window = jnp.einsum("ob,bh->ho", window_hot, bias_table, precision=highest)[:, None, :]
    attention_result, log_total = attend(query_bf, pair_all, window, head_dim)
    residual_middle = resid + mm(attention_result, w_output)
    norm_two = rms_scale(residual_middle, gain_ffn)
    logits = jnp.dot(norm_two, w_router, precision=highest)
    route_probs = jax.nn.softmax(logits, axis=-1)
    route_row = routes[0]
    slot_row = slots[0]
    route_hot = (
        route_row[:, None] == jnp.arange(logits.shape[1], dtype=jnp.int32)[None, :]
    ).astype(SINGLE)
    gate = jnp.sum(route_probs * route_hot, axis=-1)
    grad_out = cotangent[0].astype(SINGLE)
    grad_routed = (grad_out * gate[:, None]).astype(BFLOAT)
    slot_count = expert_dev * n_owner * capacity
    layout = (
        route_row // expert_dev * (expert_dev * capacity)
        + route_row % expert_dev * capacity
        + slot_row
    )
    place = jnp.where(slot_row < capacity, layout, -1)
    slot_hot = (place[:, None] == jnp.arange(slot_count, dtype=jnp.int32)[None, :]).astype(BFLOAT)
    send = mm(
        slot_hot, jnp.concatenate([norm_two.astype(BFLOAT), grad_routed], axis=1), TN
    ).astype(BFLOAT)
    returned, own_half, held_half = expert_layer(
        send.reshape(n_owner, expert_dev, capacity, 2 * width), w_in, w_out, "experts", shares, 1
    )
    returned = returned.reshape(slot_count, 2 * width)
    context = lax.axis_index("context")

    def half_sum(at):
        own = lax.dynamic_index_in_dim(own_half, at, 1, keepdims=False).astype(SINGLE)
        return own + lax.dynamic_index_in_dim(held_half, at, 1, keepdims=False).astype(SINGLE)

    expert_shares = [
        lax.ppermute(
            half_sum(context ^ step).astype(BFLOAT),
            "context",
            [(at, at ^ step) for at in range(n_context)],
        )
        for step in range(1, n_context)
    ]
    fetched = mm(slot_hot, returned)
    routed = fetched[:, :width]
    output = residual_middle + gate[:, None] * routed
    grad_gate = jnp.sum(grad_out * routed, axis=-1)
    grad_logits = grad_gate[:, None] * route_probs * (route_hot - gate[:, None])
    grad_router = jnp.einsum("td,te->de", norm_two, grad_logits, precision=highest)
    grad_norm_two = fetched[:, width:] + jnp.einsum(
        "te,de->td", grad_logits, w_router, precision=highest
    )
    grad_mid, grad_gain_ffn = jax.vjp(rms_scale, residual_middle, gain_ffn)[1](grad_norm_two)
    grad_mid = grad_mid + grad_out
    grad_attn = grad_mid.astype(BFLOAT)
    grad_output = mm(attention_result, grad_attn, TN)
    grad_attended = mm(grad_attn, w_output, NT).astype(BFLOAT)
    grad_q, grad_pair, diagonal = attend_back(
        query_bf, pair_all, grad_attended, log_total, window, head_dim
    )
    grad_query = mm(first_norm_output, grad_q, TN)
    unit = 16 * n_owner * shares
    grad_pair, early = reduce_all(
        [grad_pair.reshape(2 * seq_len, width), pack([grad_query, grad_output], unit)],
        [("context",), ("dp", "experts", "context")],
        [False, True],
        2,
    )
    grad_k, grad_v = grad_pair[:tok_count], grad_pair[tok_count:]
    grad_table = jnp.einsum("ho,ob->bh", diagonal[:, 0, :], window_hot, precision=highest)
    grad_key = mm(first_norm_output, grad_k, TN)
    grad_value = mm(first_norm_output, grad_v, TN)
    grad_norm_one = mm(grad_q, w_query, NT) + mm(grad_k, w_key, NT) + mm(grad_v, w_value, NT)
    grad_resid, grad_gain_attn = jax.vjp(rms_scale, resid, gain_attn)[1](grad_norm_one)
    grad_tokens = grad_resid + grad_mid
    grads = (grad_gain_attn, grad_gain_ffn, grad_table, grad_router)
    small = jnp.concatenate([grad.reshape(-1) for grad in grads])
    small_rows = -(-small.shape[0] // (64 * unit)) * (unit // 2)
    small = jnp.pad(small, (0, small_rows * 128 - small.shape[0])).reshape(small_rows, 128)
    late = pack([grad_key, grad_value], unit)
    cut = -(-2 * late.shape[0] // (3 * unit)) * unit
    pieces, orders = [late[:cut], small], [("dp", "context", "experts")] * 2
    if cut < late.shape[0]:
        pieces.append(late[cut:])
        orders.append(("dp", "experts", "context"))
    pieces = reduce_all(pieces, orders, [True] * len(pieces), 3)
    late = jnp.concatenate([pieces[0], *pieces[2:]], axis=0)
    summed = []
    for packed in (early, late):
        summed += [packed[:width].astype(SINGLE), packed[width : 2 * width].astype(SINGLE)]
    summed = [summed[0], summed[2], summed[3], summed[1]]
    flat, at = pieces[1].reshape(-1), 0
    for grad in grads:
        summed.append(flat[at : at + grad.size].reshape(grad.shape))
        at += grad.size
    expert_sum = half_sum(context)
    for arrived in expert_shares:
        expert_sum = expert_sum + arrived.astype(SINGLE)
    return (
        output.astype(BFLOAT)[None],
        grad_tokens[None],
        summed[0],
        summed[1],
        summed[2],
        summed[3],
        summed[4],
        summed[5],
        summed[6],
        summed[7],
        expert_sum[:, 0],
        expert_sum[:, 1].transpose(0, 2, 1),
    )


def solution(mesh):
    in_specs = (
        P(("experts", "dp"), "context", None),
        P(("experts", "dp"), "context", None),
        P(),
        P(),
        P(),
        P(),
        P(),
        P(),
        P(),
        P(),
        P("experts", None, None),
        P("experts", None, None),
        P(("experts", "dp"), "context"),
        P(("experts", "dp"), "context"),
        P(),
    )
    out_specs = (
        P(("experts", "dp"), "context", None),
        P(("experts", "dp"), "context", None),
        P(),
        P(),
        P(),
        P(),
        P(),
        P(),
        P(),
        P(),
        P("experts", None, ("context", "dp")),
        P("experts", ("context", "dp"), None),
    )
    return jax.shard_map(
        on_device, mesh=mesh, in_specs=in_specs, out_specs=out_specs, check_vma=False
    )
```
